32 devices in a mesh: groups: 2 (over y), tensor: 8 (over z, x), seq: 2 (over core).
Axes of the slice: x: 2, y: 2, z: 4, core: 2. Of those that a mesh axis runs over, the one named last changes fastest.
Arguments:
- hidden_in: bfloat16 [4, 512, 2560], P(('groups', 'seq'), 'tensor'), parts along dimension 0, may hold values from -4 to 4
- span_order: int32 [4], P('groups'), parts along dimension 0, may hold values from 0 to 7, as said below
- norm_gain: float32 [2560], replicated, may hold values from 0.5 to 2
- w_query: bfloat16 [2560, 2048], P(None, 'tensor'), may hold values from -0.125 to 0.125
- w_keyval_t: bfloat16 [2048, 2560], P('tensor'), may hold values from -0.125 to 0.125
- q_gain: float32 [128], replicated, may hold values from 0.5 to 16
- k_gain: float32 [128], replicated, may hold values from 0.5 to 16
- w_out: bfloat16 [2048, 2560], P('tensor'), may hold values from -0.5 to 0.5
Outputs:
- hidden_out: bfloat16 [4, 512, 2560], P(('groups', 'seq'), 'tensor'), parts along dimension 0
The draws below stay inside these ranges and needn't reach their ends.
There are 2 independent parts, one for each index of `groups`. The reference program is written for one: setup_inputs(seed, part) draws one part's arguments, and reference() takes and returns one part's arrays. A program takes and returns all parts, laid end to end along the dimension named above; an argument that names none is the same for every part. Nothing has to cross between parts.
Inputs may be any that keep to these rules, and one draw needn't show every extreme that they name: `span_order`: the 2 entries are different.
All inputs are finite; a program needn't handle non-finite values.
Results may differ from the reference program's by a relative error of at most 0.014.
The reference program's roundings to bfloat16 on the way count: a program that leaves them out, or rounds other values in their place, can miss the bound.
Values may be sent and summed in bfloat16 or wider, within the bound.
A program may use at most 64 MiB of HBM per device.

```python
import math
import jax
import jax.numpy as jnp
from jax import lax

D = 2560
HD = 128
KV_HEADS = 8
SPAN = 512
HEADS = 16
TOKENS = 1024
N_SEQ = 2


def spread_gain(key, upper):
    unit = jax.random.uniform(key, (HD,), dtype=jnp.float32)
    return jnp.exp(jnp.log(0.5) + unit * (jnp.log(upper) - jnp.log(0.5))).astype(jnp.float32)


def draw_hidden_in(key, part):
    key = jax.random.fold_in(key, 11)
    first_key, second_key, third_key = jax.random.split(key, 3)
    column_scale = 10.0 ** (jax.random.uniform(first_key, (D,), dtype=jnp.float32) - 1.0)
    row_scale = 10.0 ** (jax.random.uniform(second_key, (N_SEQ, SPAN, 1), dtype=jnp.float32) - 1.0)
    noise = jax.random.normal(third_key, (N_SEQ, SPAN, D), dtype=jnp.float32)
    return (jnp.clip(noise, -4.0, 4.0) * row_scale * column_scale).astype(jnp.bfloat16)


def draw_span_order(key, part):
    key = jax.random.fold_in(key, 41)
    shuffled = jax.random.permutation(key, jnp.arange(4 * N_SEQ, dtype=jnp.int32))
    return shuffled[:N_SEQ].astype(jnp.int32)


def draw_q_gain(key, part):
    key = jax.random.fold_in(key, 21)
    return spread_gain(key, 2.0)


def draw_k_gain(key, part):
    key = jax.random.fold_in(key, 31)
    return spread_gain(key, 2.0)


def shard_levels(key, dims, cuts, low, top_value):
    def one(dim, blocks):
        draws = jax.random.uniform(jax.random.fold_in(jax.random.fold_in(key, 6), dim), (blocks,), jnp.float32, low / len(cuts), top_value / len(cuts))
        return jnp.repeat(jnp.exp(draws), dims[dim] // blocks).reshape((-1,) + (1,) * (len(dims) - dim - 1))

    level = one(*cuts[0])
    for cut in cuts[1:]:
        level = level * one(*cut)
    return level


def scatter_about(key, dims, spread, reach, cuts=(), held_as=jnp.bfloat16):
    array = spread * jax.random.normal(key, dims, jnp.float32)
    if cuts:
        array = array * shard_levels(key, dims, cuts, -0.22, 0.18)
    return jnp.clip(array, -reach, reach).astype(held_as)


def setup_inputs(seed: int = 0, part: int = 0) -> dict:
    streams_of = jax.random.split(jax.random.key(seed), 9)
    part_splits = jax.random.split(jax.random.fold_in(streams_of[8], part), 9)
    return {
        "hidden_in": draw_hidden_in(jax.random.fold_in(jax.random.fold_in(streams_of[8], part), 71), part),
        "span_order": draw_span_order(jax.random.fold_in(jax.random.fold_in(streams_of[8], part), 71), part),
        "norm_gain": jnp.clip(jnp.exp(jax.random.uniform(streams_of[2], (D,), jnp.float32, math.log(0.5), math.log(2.0))), 0.5, 2.0),
        "w_query": scatter_about(streams_of[3], (D, HEADS * HD), D ** -0.5, 0.125, ((1, 8),)),
        "w_keyval_t": scatter_about(streams_of[4], (2 * KV_HEADS * HD, D), D ** -0.5, 0.125, ((0, 8),)),
        "q_gain": draw_q_gain(jax.random.fold_in(streams_of[8], 71), part),
        "k_gain": draw_k_gain(jax.random.fold_in(streams_of[8], 71), part),
        "w_out": scatter_about(streams_of[7], (HEADS * HD, D), HD ** -0.5, 0.5, ((0, 8),)),
    }


epsilon = 1e-06

def normalize(vector, gain):
    vector = vector.astype(jnp.float32)
    return vector * lax.rsqrt(lax.optimization_barrier(jnp.mean(vector * vector, axis=-1, keepdims=True)) + epsilon) * gain

def rotate(vector, position):
    half_dim = vector.shape[-1] // 2
    inverse = 1000000.0 ** (-2.0 * jnp.arange(half_dim, dtype=jnp.float32) / vector.shape[-1])
    angles = position.astype(jnp.float32)[:, None] * inverse[None, :]
    cosine = jnp.cos(angles)
    sine = jnp.sin(angles)
    front = vector[:, :half_dim]
    back = vector[:, half_dim:]
    return jnp.concatenate([front * cosine - back * sine, back * cosine + front * sine], axis=-1)

def reference(hidden_in, span_order, norm_gain, w_query, w_keyval_t, q_gain, k_gain, w_out):
    flat_rows = hidden_in.reshape(TOKENS, D)
    normed = normalize(flat_rows, norm_gain).astype(jnp.bfloat16)
    position = (span_order[:, None] * SPAN + jnp.arange(SPAN, dtype=jnp.int32)[None, :]).reshape(TOKENS).astype(jnp.int32)
    keyval = jnp.dot(normed, w_keyval_t.T, preferred_element_type=jnp.float32).astype(jnp.bfloat16)
    key_list = []
    value_list = []
    for kv_head in range(KV_HEADS):
        key_cols = keyval[:, kv_head * HD:(kv_head + 1) * HD]
        key_list.append(rotate(normalize(key_cols, k_gain), position).astype(jnp.bfloat16))
        value_list.append(keyval[:, (KV_HEADS + kv_head) * HD:(KV_HEADS + kv_head + 1) * HD])
    all_keys = jnp.stack(key_list)
    all_values = jnp.stack(value_list)
    group_size = HEADS // KV_HEADS
    visible = position[None, :] <= position[:, None]

    def one_head(head_index):
        query_cols = lax.dynamic_slice_in_dim(w_query, head_index * HD, HD, 1)
        queries = jnp.dot(normed, query_cols, preferred_element_type=jnp.float32)
        queries = (rotate(normalize(queries, q_gain), position) * HD ** (-0.5)).astype(jnp.bfloat16)
        kv_head = head_index // group_size
        scores = jnp.dot(queries, all_keys[kv_head].T, preferred_element_type=jnp.float32)
        scores = jnp.where(visible, scores, -jnp.inf)
        largest = lax.optimization_barrier(jnp.max(scores, axis=-1, keepdims=True))
        expos = jnp.exp(scores - largest)
        probs = (expos / lax.optimization_barrier(jnp.sum(expos, axis=-1, keepdims=True))).astype(jnp.bfloat16)
        return jnp.dot(probs, all_values[kv_head], preferred_element_type=jnp.float32).astype(jnp.bfloat16)

    def pair_step(total, pair_index):
        joined = jnp.concatenate([one_head(pair_index * 2), one_head(pair_index * 2 + 1)], axis=-1)
        out_rows = lax.dynamic_slice_in_dim(w_out, pair_index * 2 * HD, 2 * HD, 0)
        partial_sum = jnp.dot(joined, out_rows, preferred_element_type=jnp.float32).astype(jnp.bfloat16)
        partial_sum = lax.optimization_barrier(partial_sum)
        return (total + partial_sum.astype(jnp.float32), None)
    total, _ = lax.scan(pair_step, jnp.zeros((TOKENS, D), jnp.float32), jnp.arange(HEADS // 2, dtype=jnp.int32))
    return (flat_rows.astype(jnp.float32) + total).reshape(N_SEQ, SPAN, D).astype(jnp.bfloat16)
```

```python
import jax
import jax.numpy as jnp
import numpy as np
from jax import lax
from jax.experimental import pallas as pl
from jax.experimental.pallas import tpu as pltpu
from jax.sharding import PartitionSpec as P

HD = 128
KV_HEADS = 8


epsilon = 1e-06


def normalize(vector, gain):
    vector = vector.astype(jnp.float32)
    return vector * lax.rsqrt(jnp.mean(vector * vector, axis=-1, keepdims=True) + epsilon) * gain


def rotate(vector, position):
    half_dim = vector.shape[-1] // 2
    inverse = 1000000.0 ** (-2.0 * jnp.arange(half_dim, dtype=jnp.float32) / vector.shape[-1])
    angles = position.astype(jnp.float32)[:, None] * inverse[None, :]
    cosine = jnp.cos(angles)
    sine = jnp.sin(angles)
    front = vector[:, :half_dim]
    back = vector[:, half_dim:]
    return jnp.concatenate([front * cosine - back * sine, back * cosine + front * sine], axis=-1)


def prepare_keys(key_rows, gain, position):
    blocks = rotate(normalize(key_rows, gain), position)
    return blocks.astype(jnp.bfloat16)


def body(hidden_in, span_order, norm_gain, w_query, w_keyval_t, q_gain, k_gain, w_out):
    own_rows = hidden_in[0]
    rows_here = own_rows.shape[0]
    tensor_size = lax.axis_size("tensor")
    seq_size = lax.axis_size("seq")
    span_len = rows_here * tensor_size
    heads_here = w_query.shape[1] // HD
    group_size = heads_here * tensor_size // KV_HEADS
    kv_count = max(1, heads_here // group_size)
    own_normed = normalize(own_rows, norm_gain).astype(jnp.bfloat16)
    gathered = lax.all_gather(own_normed, "tensor", axis=0, tiled=True)
    slot_index = lax.axis_index("seq")
    offsets = jnp.arange(span_len, dtype=jnp.int32)
    position = span_order[slot_index] * span_len + offsets
    key_pos = (span_order[:, None] * span_len + offsets[None, :]).reshape(seq_size * span_len)
    query_raw = jnp.dot(gathered, w_query, preferred_element_type=jnp.float32)
    kv_columns = lax.dot_general(
        w_keyval_t, gathered, (((1,), (1,)), ((), ())), preferred_element_type=jnp.float32
    ).astype(jnp.bfloat16)
    kv_first = lax.axis_index("tensor") * heads_here // group_size
    columns = lax.all_gather(kv_columns, "tensor", axis=0, tiled=True)
    key_t = lax.dynamic_slice_in_dim(columns, kv_first * HD, kv_count * HD, 0)
    value_t = lax.dynamic_slice_in_dim(columns, (KV_HEADS + kv_first) * HD, kv_count * HD, 0)
    own_keys = prepare_keys(key_t.T, k_gain, position)
    own_values = value_t.T
    all_keys, all_values = (
        lax.all_gather(own_keys, "seq", axis=0, tiled=True),
        lax.all_gather(own_values, "seq", axis=0, tiled=True),
    )
    visible = key_pos[None, :] <= position[:, None]
    pieces = []
    for local in range(heads_here):
        query_cols = query_raw[:, local * HD : (local + 1) * HD]
        queries = (rotate(normalize(query_cols, q_gain), position) * HD ** (-0.5)).astype(
            jnp.bfloat16
        )
        scores = lax.dot_general(
            queries, all_keys, (((1,), (1,)), ((), ())), preferred_element_type=jnp.float32
        )
        scores = jnp.where(visible, scores, -jnp.inf)
        largest = jnp.max(scores, axis=-1, keepdims=True)
        expos = jnp.exp(scores - largest)
        probs = (expos / jnp.sum(expos, axis=-1, keepdims=True)).astype(jnp.bfloat16)
        pieces.append(
            jnp.dot(probs, all_values, preferred_element_type=jnp.float32).astype(jnp.bfloat16)
        )
    attended = jnp.concatenate(pieces, axis=-1)
    summed = lax.psum_scatter(
        jnp.dot(attended, w_out, preferred_element_type=jnp.float32).astype(jnp.bfloat16),
        "tensor",
        scatter_dimension=0,
        tiled=True,
    ).astype(jnp.float32)
    return (own_rows.astype(jnp.float32) + summed).astype(jnp.bfloat16)[None]


MESH = pl.DeviceIdType.MESH
Z = 4
X = 2


def layer_kernel(
    span_ref, hidden_ref, gain_ref, inverse_ref, q_gain_ref, k_gain_ref, wq_hbm, wkv_hbm, wo_hbm,
    out_ref,
    rows_ref, wq_ref, wkv_ref, wo_ref, cos_ref, sin_ref, query_ref, kv_send, kv_in, key_own, key_other,
    value_other, part_ref, x_in, up_in, down_in, line_out,
    w_sem, row_recv, row_x_send, row_line_send, row_line_send2, kv_ssem, kv_rsem, pair_ssem, pair_rsem,
    x_ssem, x_rsem, line_ssem, up_rsem, down_rsem,
):
    t = lax.axis_index("tensor")
    s = lax.axis_index("seq")
    z = t // X
    x = t % X
    block = hidden_ref.shape[0]
    chunk = X * block
    span_len = Z * chunk
    x_peer = z * X + (1 - x)
    low = z // 2
    far = z * low + (1 - low) * (3 - z)
    near = [far, 5 - far, 1, 0]
    order = [low * v + (1 - low) * (3 - v) for v in near]

    weight_copies = [
        pltpu.make_async_copy(wq_hbm, wq_ref, w_sem.at[0]),
        pltpu.make_async_copy(wkv_hbm, wkv_ref, w_sem.at[1]),
        pltpu.make_async_copy(wo_hbm, wo_ref, w_sem.at[2]),
    ]
    for copy in weight_copies:
        copy.start()

    barrier = pltpu.get_barrier_semaphore()
    for step in range(1, Z * X):
        pl.semaphore_signal(
            barrier, inc=1, device_id={"tensor": (t + step) % (Z * X)}, device_id_type=MESH
        )
    pl.semaphore_signal(barrier, inc=1, device_id={"seq": 1 - s}, device_id_type=MESH)

    own = hidden_ref[...].astype(jnp.float32)
    scale = lax.rsqrt(jnp.mean(own * own, axis=-1, keepdims=True) + epsilon)
    own_start = pl.multiple_of(t * block, block)
    rows_ref[pl.ds(own_start, block), :] = (own * scale * gain_ref[...]).astype(jnp.bfloat16)
    pl.semaphore_wait(barrier, Z * X)

    def row_copy(zb, xb, target, send_sem):
        place = pl.ds(pl.multiple_of((zb * X + xb) * block, block), block)
        return pltpu.make_async_remote_copy(
            src_ref=rows_ref.at[place, :],
            dst_ref=rows_ref.at[place, :],
            send_sem=send_sem.at[zb],
            recv_sem=row_recv.at[zb * X + xb],
            device_id={"tensor": target},
            device_id_type=MESH,
        )

    def line_up(zb):
        return row_copy(zb, x, (t + X) % (Z * X), row_line_send)

    def line_down(zb):
        return row_copy(zb, x, (t + Z * X - X) % (Z * X), row_line_send2)

    def across(zb):
        return row_copy(zb, x, x_peer, row_x_send)

    def forward(zb):
        @pl.when((zb <= z) & (z < Z - 1))
        def _():
            line_up(zb).start()

        @pl.when((zb >= z) & (z > 0))
        def _():
            line_down(zb).start()

        across(zb).start()

    forward(z)

    inverse = inverse_ref[...]
    position = span_ref[s] * span_len + lax.broadcasted_iota(jnp.int32, (span_len, HD), 0)
    angles = position.astype(jnp.float32) * inverse
    cos_ref[...] = jnp.cos(angles)
    lane = lax.broadcasted_iota(jnp.int32, (span_len, HD), 1)
    sine = jnp.sin(angles)
    sin_ref[...] = jnp.where(lane < HD // 2, -sine, sine)

    def norm_rotate(v, gain, zb):
        place = pl.ds(pl.multiple_of(zb * chunk, chunk), chunk)
        v = v * lax.rsqrt(jnp.mean(v * v, axis=-1, keepdims=True) + epsilon) * gain
        return v * cos_ref[place, :] + pltpu.roll(v, HD // 2, 1) * sin_ref[place, :]

    kind = t // Z

    def kv_copy(zb, j):
        return pltpu.make_async_remote_copy(
            src_ref=kv_send.at[zb, j],
            dst_ref=kv_in.at[kind, pl.ds(pl.multiple_of(zb * chunk, chunk), chunk), :],
            send_sem=kv_ssem.at[zb, j],
            recv_sem=kv_rsem.at[kind, zb],
            device_id={"tensor": (2 * t + j) % (Z * X)},
            device_id_type=MESH,
        )

    def project(zb):
        place = pl.ds(pl.multiple_of(zb * chunk, chunk), chunk)
        rows = rows_ref[place, :]
        kv = lax.dot_general(
            rows, wkv_ref[...], (((1,), (1,)), ((), ())), preferred_element_type=jnp.float32
        ).astype(jnp.bfloat16)
        for j in range(2):
            kv_send[zb, j] = kv[:, j * HD : (j + 1) * HD]
            here = (2 * t + j) % (Z * X) == t

            @pl.when(here)
            def _():
                kv_in[kind, place, :] = kv_send[zb, j]

            @pl.when(jnp.logical_not(here))
            def _():
                kv_copy(zb, j).start()

        raw = jnp.dot(rows, wq_ref[...], preferred_element_type=jnp.float32)
        for j in range(2):
            q = norm_rotate(raw[:, j * HD : (j + 1) * HD], q_gain_ref[...], zb) * HD ** (-0.5)
            query_ref[zb, j * chunk : (j + 1) * chunk, :] = q.astype(jnp.bfloat16)

    weight_copies[1].wait()
    weight_copies[0].wait()
    for k in range(1, Z):
        zb = order[k]
        row_copy(zb, x, x_peer, row_x_send).wait_recv()
        forward(zb)
        row_copy(order[k - 1], 1 - x, x_peer, row_x_send).wait_recv()
        project(order[k - 1])
    row_copy(order[Z - 1], 1 - x, x_peer, row_x_send).wait_recv()
    project(order[Z - 1])

    def pair_copy(index, zb, source, target):
        place = pl.ds(zb * chunk, chunk)
        return pltpu.make_async_remote_copy(
            src_ref=source.at[place, :],
            dst_ref=target.at[place, :],
            send_sem=pair_ssem.at[index, zb],
            recv_sem=pair_rsem.at[index, zb],
            device_id={"seq": 1 - s},
            device_id_type=MESH,
        )

    def kv_arrived(which, zb):
        @pl.when((t // 2 + which * Z) != t)
        def _():
            pltpu.make_async_remote_copy(
                src_ref=kv_send.at[zb, 0],
                dst_ref=kv_in.at[which, pl.ds(zb * chunk, chunk), :],
                send_sem=kv_ssem.at[zb, 0],
                recv_sem=kv_rsem.at[which, zb],
                device_id={"tensor": x_peer},
                device_id_type=MESH,
            ).wait_recv()

    values = kv_in.at[1]
    for zb in range(Z):
        kv_arrived(0, zb)
        place = slice(zb * chunk, (zb + 1) * chunk)
        raw = kv_in[0, place, :].astype(jnp.float32)
        key_own[place, :] = norm_rotate(raw, k_gain_ref[...], zb).astype(jnp.bfloat16)
        pair_copy(0, zb, key_own, key_other).start()
        kv_arrived(1, zb)
        pair_copy(1, zb, values, value_other).start()
    weight_copies[2].wait()
    for zb in range(Z):
        pair_copy(0, zb, key_own, key_other).wait_recv()
        pair_copy(1, zb, values, value_other).wait_recv()

    hide = jnp.where(span_ref[1 - s] < span_ref[s], 0.0, -1e30).astype(jnp.float32)

    def attend(zb):
        q = query_ref[zb]
        nt = (((1,), (1,)), ((), ()))
        mine = lax.dot_general(q, key_own[...], nt, preferred_element_type=jnp.float32)
        others = lax.dot_general(q, key_other[...], nt, preferred_element_type=jnp.float32) + hide
        row = lax.broadcasted_iota(jnp.int32, mine.shape, 0) % chunk + zb * chunk
        column = lax.broadcasted_iota(jnp.int32, mine.shape, 1)
        mine = jnp.where(column <= row, mine, -jnp.inf)
        largest = jnp.maximum(
            jnp.max(mine, axis=-1, keepdims=True), jnp.max(others, axis=-1, keepdims=True)
        )
        mine = jnp.exp(mine - largest)
        others = jnp.exp(others - largest)
        total = jnp.sum(mine, axis=-1, keepdims=True) + jnp.sum(others, axis=-1, keepdims=True)
        share = 1.0 / total
        result = jnp.dot(
            (mine * share).astype(jnp.bfloat16), kv_in[1], preferred_element_type=jnp.float32
        ) + jnp.dot(
            (others * share).astype(jnp.bfloat16), value_other[...], preferred_element_type=jnp.float32
        )
        result = result.astype(jnp.bfloat16)
        joined = jnp.concatenate([result[:chunk], result[chunk:]], axis=-1)
        part_ref[zb] = jnp.dot(joined, wo_ref[...], preferred_element_type=jnp.float32).astype(
            jnp.bfloat16
        )

    def part_copy(zb):
        place = pl.ds(pl.multiple_of((1 - x) * block, block), block)
        return pltpu.make_async_remote_copy(
            src_ref=part_ref.at[zb, place, :],
            dst_ref=x_in.at[zb],
            send_sem=x_ssem.at[zb],
            recv_sem=x_rsem.at[zb],
            device_id={"tensor": x_peer},
            device_id_type=MESH,
        )

    def sum_up(zb):
        return pltpu.make_async_remote_copy(
            src_ref=line_out.at[zb], dst_ref=up_in.at[zb], send_sem=line_ssem.at[zb],
            recv_sem=up_rsem.at[zb], device_id={"tensor": (t + X) % (Z * X)}, device_id_type=MESH,
        )

    def sum_down(zb):
        return pltpu.make_async_remote_copy(
            src_ref=line_out.at[zb], dst_ref=down_in.at[zb], send_sem=line_ssem.at[zb],
            recv_sem=down_rsem.at[zb], device_id={"tensor": (t + Z * X - X) % (Z * X)},
            device_id_type=MESH,
        )

    back = order[::-1]
    for zb in back:
        attend(zb)
        part_copy(zb).start()

    own_half = pl.ds(pl.multiple_of(x * block, block), block)

    def pair_sum(zb):
        return part_ref[zb, own_half, :].astype(jnp.float32) + x_in[zb].astype(jnp.float32)

    for zb in back[: Z - 1]:
        part_copy(zb).wait_recv()

        @pl.when(zb > z)
        def _():
            @pl.when(z > 0)
            def _():
                sum_up(zb).wait_recv()
                line_out[zb] = (pair_sum(zb) + up_in[zb].astype(jnp.float32)).astype(jnp.bfloat16)

            @pl.when(z == 0)
            def _():
                line_out[zb] = pair_sum(zb).astype(jnp.bfloat16)

            sum_up(zb).start()

        @pl.when(zb < z)
        def _():
            @pl.when(z < Z - 1)
            def _():
                sum_down(zb).wait_recv()
                line_out[zb] = (pair_sum(zb) + down_in[zb].astype(jnp.float32)).astype(jnp.bfloat16)

            @pl.when(z == Z - 1)
            def _():
                line_out[zb] = pair_sum(zb).astype(jnp.bfloat16)

            sum_down(zb).start()

    part_copy(z).wait_recv()
    total = hidden_ref[...].astype(jnp.float32) + pair_sum(z)

    @pl.when(z == 0)
    def _():
        sum_down(z).wait_recv()
        out_ref[...] = (total + down_in[z].astype(jnp.float32)).astype(jnp.bfloat16)

    @pl.when(z == Z - 1)
    def _():
        sum_up(z).wait_recv()
        out_ref[...] = (total + up_in[z].astype(jnp.float32)).astype(jnp.bfloat16)

    @pl.when((z > 0) & (z < Z - 1))
    def _():
        sum_down(z).wait_recv()
        sum_up(z).wait_recv()
        out_ref[...] = (
            total + down_in[z].astype(jnp.float32) + up_in[z].astype(jnp.float32)
        ).astype(jnp.bfloat16)

    for zb in range(Z):
        across(zb).wait_send()
        part_copy(zb).wait_send()
        pair_copy(0, zb, key_own, key_other).wait_send()
        pair_copy(1, zb, values, value_other).wait_send()

        @pl.when((zb <= z) & (z < Z - 1))
        def _():
            line_up(zb).wait_send()

        @pl.when((zb >= z) & (z > 0))
        def _():
            line_down(zb).wait_send()

        @pl.when(zb != z)
        def _():
            sum_up(zb).wait_send()

        for j in range(2):
            @pl.when((2 * t + j) % (Z * X) != t)
            def _():
                kv_copy(zb, j).wait_send()


def fused_body(hidden_in, span_order, norm_gain, w_query, w_keyval_t, q_gain, k_gain, w_out):
    _, block, width = hidden_in.shape
    chunk = X * block
    span_len = Z * chunk
    inverse = 1000000.0 ** (-2.0 * np.arange(HD // 2) / HD)
    inverse = jnp.asarray(np.concatenate([inverse, inverse])[None], jnp.float32)
    vmem = pl.BlockSpec(memory_space=pltpu.VMEM)
    anywhere = pl.BlockSpec(memory_space=pl.ANY)
    bf16 = jnp.bfloat16
    dma = pltpu.SemaphoreType.DMA
    out = pl.pallas_call(
        layer_kernel,
        out_shape=jax.ShapeDtypeStruct((block, width), bf16),
        in_specs=[pl.BlockSpec(memory_space=pltpu.SMEM)] + [vmem] * 5 + [anywhere] * 3,
        out_specs=vmem,
        scratch_shapes=[
            pltpu.VMEM((span_len, width), bf16),
            pltpu.VMEM(w_query.shape, bf16),
            pltpu.VMEM(w_keyval_t.shape, bf16),
            pltpu.VMEM(w_out.shape, bf16),
            pltpu.VMEM((span_len, HD), jnp.float32),
            pltpu.VMEM((span_len, HD), jnp.float32),
            pltpu.VMEM((Z, 2 * chunk, HD), bf16),
            pltpu.VMEM((Z, 2, chunk, HD), bf16),
            pltpu.VMEM((2, span_len, HD), bf16),
            pltpu.VMEM((span_len, HD), bf16),
            pltpu.VMEM((span_len, HD), bf16),
            pltpu.VMEM((span_len, HD), bf16),
            pltpu.VMEM((Z, chunk, width), bf16),
            pltpu.VMEM((Z, block, width), bf16),
            pltpu.VMEM((Z, block, width), bf16),
            pltpu.VMEM((Z, block, width), bf16),
            pltpu.VMEM((Z, block, width), bf16),
            dma((3,)),
            dma((Z * X,)),
            dma((Z,)),
            dma((Z,)),
            dma((Z,)),
            dma((Z, 2)),
            dma((2, Z)),
            dma((2, Z)),
            dma((2, Z)),
            dma((Z,)),
            dma((Z,)),
            dma((Z,)),
            dma((Z,)),
            dma((Z,)),
        ],
        compiler_params=pltpu.CompilerParams(
            collective_id=0, has_side_effects=True, vmem_limit_bytes=48 * 1024 * 1024
        ),
    )(
        span_order, hidden_in[0], norm_gain[None], inverse, q_gain[None], k_gain[None],
        w_query, w_keyval_t, w_out,
    )
    return out[None]


def solution(mesh):
    placed = (
        P(("groups", "seq"), "tensor", None),
        P("groups"),
        P(),
        P(None, "tensor"),
        P("tensor", None),
        P(),
        P(),
        P("tensor", None),
    )
    def chosen(hidden_in, span_order, norm_gain, w_query, *rest):
        fits = (
            mesh.shape["tensor"] == Z * X
            and mesh.shape["seq"] == 2
            and w_query.shape[1] == 2 * HD
            and hidden_in.shape[1] % 16 == 0
        )
        run = fused_body if fits else body
        return run(hidden_in, span_order, norm_gain, w_query, *rest)

    return jax.shard_map(
        chosen,
        mesh=mesh,
        in_specs=placed,
        out_specs=P(("groups", "seq"), "tensor", None),
        check_vma=False,
    )
```

```python
import math
import jax
import jax.numpy as jnp
from jax import lax
from jax.experimental import pallas as pl
from jax.experimental.pallas import tpu as pltpu
from jax.sharding import PartitionSpec as P

HD = 128
KV_HEADS = 8


epsilon = 1e-06


def normalize(vector, gain):
    vector = vector.astype(jnp.float32)
    return vector * lax.rsqrt(jnp.mean(vector * vector, axis=-1, keepdims=True) + epsilon) * gain


def rotate(vector, position):
    half_dim = vector.shape[-1] // 2
    inverse = 1000000.0 ** (-2.0 * jnp.arange(half_dim, dtype=jnp.float32) / vector.shape[-1])
    angles = position.astype(jnp.float32)[:, None] * inverse[None, :]
    cosine = jnp.cos(angles)
    sine = jnp.sin(angles)
    front = vector[:, :half_dim]
    back = vector[:, half_dim:]
    return jnp.concatenate([front * cosine - back * sine, back * cosine + front * sine], axis=-1)


def prepare_keys(key_rows, gain, position):
    blocks = rotate(normalize(key_rows, gain), position)
    return blocks.astype(jnp.bfloat16)


def body(hidden_in, span_order, norm_gain, w_query, w_keyval_t, q_gain, k_gain, w_out):
    own_rows = hidden_in[0]
    rows_here = own_rows.shape[0]
    tensor_size = lax.axis_size("tensor")
    seq_size = lax.axis_size("seq")
    span_len = rows_here * tensor_size
    heads_here = w_query.shape[1] // HD
    group_size = heads_here * tensor_size // KV_HEADS
    kv_count = max(1, heads_here // group_size)
    own_normed = normalize(own_rows, norm_gain).astype(jnp.bfloat16)
    gathered = lax.all_gather(own_normed, "tensor", axis=0, tiled=True)
    slot_index = lax.axis_index("seq")
    offsets = jnp.arange(span_len, dtype=jnp.int32)
    position = span_order[slot_index] * span_len + offsets
    key_pos = (span_order[:, None] * span_len + offsets[None, :]).reshape(seq_size * span_len)
    query_raw = jnp.dot(gathered, w_query, preferred_element_type=jnp.float32)
    kv_columns = lax.dot_general(
        w_keyval_t, gathered, (((1,), (1,)), ((), ())), preferred_element_type=jnp.float32
    ).astype(jnp.bfloat16)
    kv_first = lax.axis_index("tensor") * heads_here // group_size
    columns = lax.all_gather(kv_columns, "tensor", axis=0, tiled=True)
    key_t = lax.dynamic_slice_in_dim(columns, kv_first * HD, kv_count * HD, 0)
    value_t = lax.dynamic_slice_in_dim(columns, (KV_HEADS + kv_first) * HD, kv_count * HD, 0)
    own_keys = prepare_keys(key_t.T, k_gain, position)
    own_values = value_t.T
    all_keys, all_values = (
        lax.all_gather(own_keys, "seq", axis=0, tiled=True),
        lax.all_gather(own_values, "seq", axis=0, tiled=True),
    )
    visible = key_pos[None, :] <= position[:, None]
    pieces = []
    for local in range(heads_here):
        query_cols = query_raw[:, local * HD : (local + 1) * HD]
        queries = (rotate(normalize(query_cols, q_gain), position) * HD ** (-0.5)).astype(
            jnp.bfloat16
        )
        scores = lax.dot_general(
            queries, all_keys, (((1,), (1,)), ((), ())), preferred_element_type=jnp.float32
        )
        scores = jnp.where(visible, scores, -jnp.inf)
        largest = jnp.max(scores, axis=-1, keepdims=True)
        expos = jnp.exp(scores - largest)
        probs = (expos / jnp.sum(expos, axis=-1, keepdims=True)).astype(jnp.bfloat16)
        pieces.append(
            jnp.dot(probs, all_values, preferred_element_type=jnp.float32).astype(jnp.bfloat16)
        )
    attended = jnp.concatenate(pieces, axis=-1)
    summed = lax.psum_scatter(
        jnp.dot(attended, w_out, preferred_element_type=jnp.float32).astype(jnp.bfloat16),
        "tensor",
        scatter_dimension=0,
        tiled=True,
    ).astype(jnp.float32)
    return (own_rows.astype(jnp.float32) + summed).astype(jnp.bfloat16)[None]


MESH = pl.DeviceIdType.MESH
Z = 4
X = 2


def layer_kernel(
    span_hbm, hidden_hbm, gain_hbm, q_gain_hbm, k_gain_hbm, wq_hbm, wkv_hbm, wo_hbm,
    out_ref,
    span_ref, hidden_ref, gain_ref, q_gain_ref, k_gain_ref, wkv_t_ref,
    rows_ref, wq_ref, wkv_ref, wo_ref, cos_ref, sin_ref, query_ref, kv_send, kv_in, key_own, key_other,
    value_other, part_ref, x_in, up_in, down_in, line_out,
    w_sem, row_recv, row_x_send, row_line_send, row_line_send2, kv_ssem, kv_rsem, pair_ssem, pair_rsem,
    x_ssem, x_rsem, line_ssem, up_rsem, down_rsem,
):
    t = lax.axis_index("tensor")
    s = lax.axis_index("seq")
    z = t // X
    x = t % X
    block = hidden_hbm.shape[1]
    chunk = X * block
    span_len = Z * chunk
    x_peer = z * X + (1 - x)
    low = z // 2
    far = z * low + (1 - low) * (3 - z)
    near = [far, 5 - far, 1, 0]
    order = [low * v + (1 - low) * (3 - v) for v in near]

    small_copies = [
        pltpu.make_async_copy(source, target, w_sem.at[3 + i])
        for i, (source, target) in enumerate([
            (hidden_hbm.at[0], hidden_ref), (gain_hbm, gain_ref), (span_hbm, span_ref),
            (q_gain_hbm, q_gain_ref), (k_gain_hbm, k_gain_ref),
        ])
    ]
    for copy in small_copies:
        copy.start()
    weight_copies = [
        pltpu.make_async_copy(wq_hbm, wq_ref, w_sem.at[0]),
        pltpu.make_async_copy(wkv_hbm, wkv_ref, w_sem.at[1]),
        pltpu.make_async_copy(wo_hbm, wo_ref, w_sem.at[2]),
    ]
    barrier = pltpu.get_barrier_semaphore()
    for step in range(1, Z * X):
        pl.semaphore_signal(
            barrier, inc=1, device_id={"tensor": (t + step) % (Z * X)}, device_id_type=MESH
        )
    pl.semaphore_signal(barrier, inc=1, device_id={"seq": 1 - s}, device_id_type=MESH)

    small_copies[0].wait()
    small_copies[1].wait()
    own = hidden_ref[...].astype(jnp.float32)
    scale = lax.rsqrt(jnp.mean(own * own, axis=-1, keepdims=True) + epsilon)
    own_start = pl.multiple_of(t * block, block)
    rows_ref[pl.ds(own_start, block), :] = (own * scale * gain_ref[...][None]).astype(jnp.bfloat16)
    pl.semaphore_wait(barrier, Z * X)

    def row_copy(zb, xb, target, send_sem):
        place = pl.ds(pl.multiple_of((zb * X + xb) * block, block), block)
        return pltpu.make_async_remote_copy(
            src_ref=rows_ref.at[place, :],
            dst_ref=rows_ref.at[place, :],
            send_sem=send_sem.at[zb],
            recv_sem=row_recv.at[zb * X + xb],
            device_id={"tensor": target},
            device_id_type=MESH,
        )

    def line_up(zb):
        return row_copy(zb, x, (t + X) % (Z * X), row_line_send)

    def line_down(zb):
        return row_copy(zb, x, (t + Z * X - X) % (Z * X), row_line_send2)

    def across(zb):
        return row_copy(zb, x, x_peer, row_x_send)

    def forward(zb):
        @pl.when((zb <= z) & (z < Z - 1))
        def _():
            line_up(zb).start()

        @pl.when((zb >= z) & (z > 0))
        def _():
            line_down(zb).start()

        across(zb).start()

    forward(z)
    for copy in weight_copies:
        copy.start()
    for copy in small_copies[2:]:
        copy.wait()
    power = lax.broadcasted_iota(jnp.int32, (1, HD), 1) % (HD // 2)
    inverse = jnp.exp(power.astype(jnp.float32) * (-math.log(1000000.0) / (HD // 2)))
    position = span_ref[s] * span_len + lax.broadcasted_iota(jnp.int32, (span_len, HD), 0)
    angles = position.astype(jnp.float32) * inverse
    cos_ref[...] = jnp.cos(angles)
    lane = lax.broadcasted_iota(jnp.int32, (span_len, HD), 1)
    sine = jnp.sin(angles)
    sin_ref[...] = jnp.where(lane < HD // 2, -sine, sine)

    def norm_rotate(v, gain, zb):
        place = pl.ds(pl.multiple_of(zb * chunk, chunk), chunk)
        v = v * lax.rsqrt(jnp.mean(v * v, axis=-1, keepdims=True) + epsilon) * gain
        return v * cos_ref[place, :] + pltpu.roll(v, HD // 2, 1) * sin_ref[place, :]

    kind = t // Z

    def kv_copy(zb, j):
        return pltpu.make_async_remote_copy(
            src_ref=kv_send.at[zb, j],
            dst_ref=kv_in.at[kind, pl.ds(pl.multiple_of(zb * chunk, chunk), chunk), :],
            send_sem=kv_ssem.at[zb, j],
            recv_sem=kv_rsem.at[kind, zb],
            device_id={"tensor": (2 * t + j) % (Z * X)},
            device_id_type=MESH,
        )

    def project(zb):
        place = pl.ds(pl.multiple_of(zb * chunk, chunk), chunk)
        rows = rows_ref[place, :]
        kv = jnp.dot(rows, wkv_t_ref[...], preferred_element_type=jnp.float32).astype(jnp.bfloat16)
        for j in range(2):
            kv_send[zb, j] = kv[:, j * HD : (j + 1) * HD]
            here = (2 * t + j) % (Z * X) == t

            @pl.when(here)
            def _():
                kv_in[kind, place, :] = kv_send[zb, j]

            @pl.when(jnp.logical_not(here))
            def _():
                kv_copy(zb, j).start()

        raw = jnp.dot(rows, wq_ref[...], preferred_element_type=jnp.float32)
        for j in range(2):
            q = norm_rotate(raw[:, j * HD : (j + 1) * HD], q_gain_ref[...][None], zb) * HD ** (-0.5)
            query_ref[zb, j * chunk : (j + 1) * chunk, :] = q.astype(jnp.bfloat16)

    weight_copies[1].wait()
    wkv_t_ref[...] = wkv_ref[...].T
    weight_copies[0].wait()
    for k in range(1, Z):
        zb = order[k]
        row_copy(zb, x, x_peer, row_x_send).wait_recv()
        forward(zb)
        row_copy(order[k - 1], 1 - x, x_peer, row_x_send).wait_recv()
        project(order[k - 1])
    row_copy(order[Z - 1], 1 - x, x_peer, row_x_send).wait_recv()
    project(order[Z - 1])

    def pair_copy(index, zb, source, target):
        place = pl.ds(zb * chunk, chunk)
        return pltpu.make_async_remote_copy(
            src_ref=source.at[place, :],
            dst_ref=target.at[place, :],
            send_sem=pair_ssem.at[index, zb],
            recv_sem=pair_rsem.at[index, zb],
            device_id={"seq": 1 - s},
            device_id_type=MESH,
        )

    def kv_arrived(which, zb):
        @pl.when((t // 2 + which * Z) != t)
        def _():
            pltpu.make_async_remote_copy(
                src_ref=kv_send.at[zb, 0],
                dst_ref=kv_in.at[which, pl.ds(zb * chunk, chunk), :],
                send_sem=kv_ssem.at[zb, 0],
                recv_sem=kv_rsem.at[which, zb],
                device_id={"tensor": x_peer},
                device_id_type=MESH,
            ).wait_recv()

    values = kv_in.at[1]
    for zb in range(Z):
        kv_arrived(0, zb)
        place = slice(zb * chunk, (zb + 1) * chunk)
        raw = kv_in[0, place, :].astype(jnp.float32)
        key_own[place, :] = norm_rotate(raw, k_gain_ref[...][None], zb).astype(jnp.bfloat16)
        pair_copy(0, zb, key_own, key_other).start()
        kv_arrived(1, zb)
        pair_copy(1, zb, values, value_other).start()
    weight_copies[2].wait()
    for zb in range(Z):
        pair_copy(0, zb, key_own, key_other).wait_recv()
        pair_copy(1, zb, values, value_other).wait_recv()

    hide = jnp.where(span_ref[1 - s] < span_ref[s], 0.0, -1e30).astype(jnp.float32)

    def attend(zb):
        q = query_ref[zb]
        nt = (((1,), (1,)), ((), ()))
        mine = lax.dot_general(q, key_own[...], nt, preferred_element_type=jnp.float32)
        others = lax.dot_general(q, key_other[...], nt, preferred_element_type=jnp.float32) + hide
        row = lax.broadcasted_iota(jnp.int32, mine.shape, 0) % chunk + zb * chunk
        column = lax.broadcasted_iota(jnp.int32, mine.shape, 1)
        mine = jnp.where(column <= row, mine, -jnp.inf)
        largest = jnp.maximum(
            jnp.max(mine, axis=-1, keepdims=True), jnp.max(others, axis=-1, keepdims=True)
        )
        mine = jnp.exp(mine - largest)
        others = jnp.exp(others - largest)
        total = jnp.sum(mine, axis=-1, keepdims=True) + jnp.sum(others, axis=-1, keepdims=True)
        share = 1.0 / total
        result = jnp.dot(
            (mine * share).astype(jnp.bfloat16), kv_in[1], preferred_element_type=jnp.float32
        ) + jnp.dot(
            (others * share).astype(jnp.bfloat16), value_other[...], preferred_element_type=jnp.float32
        )
        result = result.astype(jnp.bfloat16)
        joined = jnp.concatenate([result[:chunk], result[chunk:]], axis=-1)
        part_ref[zb] = jnp.dot(joined, wo_ref[...], preferred_element_type=jnp.float32).astype(
            jnp.bfloat16
        )

    def part_copy(zb):
        place = pl.ds(pl.multiple_of((1 - x) * block, block), block)
        return pltpu.make_async_remote_copy(
            src_ref=part_ref.at[zb, place, :],
            dst_ref=x_in.at[zb],
            send_sem=x_ssem.at[zb],
            recv_sem=x_rsem.at[zb],
            device_id={"tensor": x_peer},
            device_id_type=MESH,
        )

    def sum_up(zb):
        return pltpu.make_async_remote_copy(
            src_ref=line_out.at[zb], dst_ref=up_in.at[zb], send_sem=line_ssem.at[zb],
            recv_sem=up_rsem.at[zb], device_id={"tensor": (t + X) % (Z * X)}, device_id_type=MESH,
        )

    def sum_down(zb):
        return pltpu.make_async_remote_copy(
            src_ref=line_out.at[zb], dst_ref=down_in.at[zb], send_sem=line_ssem.at[zb],
            recv_sem=down_rsem.at[zb], device_id={"tensor": (t + Z * X - X) % (Z * X)},
            device_id_type=MESH,
        )

    back = order[::-1]
    for zb in back:
        attend(zb)
        part_copy(zb).start()

    own_half = pl.ds(pl.multiple_of(x * block, block), block)

    def pair_sum(zb):
        return part_ref[zb, own_half, :].astype(jnp.float32) + x_in[zb].astype(jnp.float32)

    for zb in back[: Z - 1]:
        part_copy(zb).wait_recv()

        @pl.when(zb > z)
        def _():
            @pl.when(z > 0)
            def _():
                sum_up(zb).wait_recv()
                line_out[zb] = (pair_sum(zb) + up_in[zb].astype(jnp.float32)).astype(jnp.bfloat16)

            @pl.when(z == 0)
            def _():
                line_out[zb] = pair_sum(zb).astype(jnp.bfloat16)

            sum_up(zb).start()

        @pl.when(zb < z)
        def _():
            @pl.when(z < Z - 1)
            def _():
                sum_down(zb).wait_recv()
                line_out[zb] = (pair_sum(zb) + down_in[zb].astype(jnp.float32)).astype(jnp.bfloat16)

            @pl.when(z == Z - 1)
            def _():
                line_out[zb] = pair_sum(zb).astype(jnp.bfloat16)

            sum_down(zb).start()

    part_copy(z).wait_recv()
    total = hidden_ref[...].astype(jnp.float32) + pair_sum(z)

    @pl.when(z == 0)
    def _():
        sum_down(z).wait_recv()
        out_ref[...] = (total + down_in[z].astype(jnp.float32)).astype(jnp.bfloat16)

    @pl.when(z == Z - 1)
    def _():
        sum_up(z).wait_recv()
        out_ref[...] = (total + up_in[z].astype(jnp.float32)).astype(jnp.bfloat16)

    @pl.when((z > 0) & (z < Z - 1))
    def _():
        sum_down(z).wait_recv()
        sum_up(z).wait_recv()
        out_ref[...] = (
            total + down_in[z].astype(jnp.float32) + up_in[z].astype(jnp.float32)
        ).astype(jnp.bfloat16)

    for zb in range(Z):
        across(zb).wait_send()
        part_copy(zb).wait_send()
        pair_copy(0, zb, key_own, key_other).wait_send()
        pair_copy(1, zb, values, value_other).wait_send()

        @pl.when((zb <= z) & (z < Z - 1))
        def _():
            line_up(zb).wait_send()

        @pl.when((zb >= z) & (z > 0))
        def _():
            line_down(zb).wait_send()

        @pl.when(zb != z)
        def _():
            sum_up(zb).wait_send()

        for j in range(2):
            @pl.when((2 * t + j) % (Z * X) != t)
            def _():
                kv_copy(zb, j).wait_send()


def fused_body(hidden_in, span_order, norm_gain, w_query, w_keyval_t, q_gain, k_gain, w_out):
    _, block, width = hidden_in.shape
    chunk = X * block
    span_len = Z * chunk
    vmem = pl.BlockSpec(memory_space=pltpu.VMEM)
    hbm = pl.BlockSpec(memory_space=pltpu.HBM)
    bf16 = jnp.bfloat16
    dma = pltpu.SemaphoreType.DMA
    out = pl.pallas_call(
        layer_kernel,
        out_shape=jax.ShapeDtypeStruct((block, width), bf16),
        in_specs=[hbm] * 8,
        out_specs=vmem,
        scratch_shapes=[
            pltpu.SMEM(span_order.shape, jnp.int32),
            pltpu.VMEM((block, width), bf16),
            pltpu.VMEM(norm_gain.shape, jnp.float32),
            pltpu.VMEM(q_gain.shape, jnp.float32),
            pltpu.VMEM(k_gain.shape, jnp.float32),
            pltpu.VMEM((width, w_keyval_t.shape[0]), bf16),
            pltpu.VMEM((span_len, width), bf16),
            pltpu.VMEM(w_query.shape, bf16),
            pltpu.VMEM(w_keyval_t.shape, bf16),
            pltpu.VMEM(w_out.shape, bf16),
            pltpu.VMEM((span_len, HD), jnp.float32),
            pltpu.VMEM((span_len, HD), jnp.float32),
            pltpu.VMEM((Z, 2 * chunk, HD), bf16),
            pltpu.VMEM((Z, 2, chunk, HD), bf16),
            pltpu.VMEM((2, span_len, HD), bf16),
            pltpu.VMEM((span_len, HD), bf16),
            pltpu.VMEM((span_len, HD), bf16),
            pltpu.VMEM((span_len, HD), bf16),
            pltpu.VMEM((Z, chunk, width), bf16),
            pltpu.VMEM((Z, block, width), bf16),
            pltpu.VMEM((Z, block, width), bf16),
            pltpu.VMEM((Z, block, width), bf16),
            pltpu.VMEM((Z, block, width), bf16),
            dma((8,)),
            dma((Z * X,)),
            dma((Z,)),
            dma((Z,)),
            dma((Z,)),
            dma((Z, 2)),
            dma((2, Z)),
            dma((2, Z)),
            dma((2, Z)),
            dma((Z,)),
            dma((Z,)),
            dma((Z,)),
            dma((Z,)),
            dma((Z,)),
        ],
        compiler_params=pltpu.CompilerParams(
            collective_id=0, has_side_effects=True, vmem_limit_bytes=48 * 1024 * 1024
        ),
    )(
        span_order, hidden_in, norm_gain, q_gain, k_gain,
        w_query, w_keyval_t, w_out,
    )
    return out[None]


def solution(mesh):
    placed = (
        P(("groups", "seq"), "tensor", None),
        P("groups"),
        P(),
        P(None, "tensor"),
        P("tensor", None),
        P(),
        P(),
        P("tensor", None),
    )
    def chosen(hidden_in, span_order, norm_gain, w_query, *rest):
        fits = (
            mesh.shape["tensor"] == Z * X
            and mesh.shape["seq"] == 2
            and w_query.shape[1] == 2 * HD
            and hidden_in.shape[1] % 16 == 0
        )
        run = fused_body if fits else body
        return run(hidden_in, span_order, norm_gain, w_query, *rest)

    return jax.shard_map(
        chosen,
        mesh=mesh,
        in_specs=placed,
        out_specs=P(("groups", "seq"), "tensor", None),
        check_vma=False,
    )
```

```python
import math
import jax
import jax.numpy as jnp
from jax import lax
from jax.experimental import pallas as pl
from jax.experimental.pallas import tpu as pltpu
from jax.sharding import PartitionSpec as P

HD = 128
KV_HEADS = 8


epsilon = 1e-06


def normalize(vector, gain):
    vector = vector.astype(jnp.float32)
    return vector * lax.rsqrt(jnp.mean(vector * vector, axis=-1, keepdims=True) + epsilon) * gain


def rotate(vector, position):
    half_dim = vector.shape[-1] // 2
    inverse = 1000000.0 ** (-2.0 * jnp.arange(half_dim, dtype=jnp.float32) / vector.shape[-1])
    angles = position.astype(jnp.float32)[:, None] * inverse[None, :]
    cosine = jnp.cos(angles)
    sine = jnp.sin(angles)
    front = vector[:, :half_dim]
    back = vector[:, half_dim:]
    return jnp.concatenate([front * cosine - back * sine, back * cosine + front * sine], axis=-1)


def prepare_keys(key_rows, gain, position):
    blocks = rotate(normalize(key_rows, gain), position)
    return blocks.astype(jnp.bfloat16)


def body(hidden_in, span_order, norm_gain, w_query, w_keyval_t, q_gain, k_gain, w_out):
    own_rows = hidden_in[0]
    rows_here = own_rows.shape[0]
    tensor_size = lax.axis_size("tensor")
    seq_size = lax.axis_size("seq")
    span_len = rows_here * tensor_size
    heads_here = w_query.shape[1] // HD
    group_size = heads_here * tensor_size // KV_HEADS
    kv_count = max(1, heads_here // group_size)
    own_normed = normalize(own_rows, norm_gain).astype(jnp.bfloat16)
    gathered = lax.all_gather(own_normed, "tensor", axis=0, tiled=True)
    slot_index = lax.axis_index("seq")
    offsets = jnp.arange(span_len, dtype=jnp.int32)
    position = span_order[slot_index] * span_len + offsets
    key_pos = (span_order[:, None] * span_len + offsets[None, :]).reshape(seq_size * span_len)
    query_raw = jnp.dot(gathered, w_query, preferred_element_type=jnp.float32)
    kv_columns = lax.dot_general(
        w_keyval_t, gathered, (((1,), (1,)), ((), ())), preferred_element_type=jnp.float32
    ).astype(jnp.bfloat16)
    kv_first = lax.axis_index("tensor") * heads_here // group_size
    columns = lax.all_gather(kv_columns, "tensor", axis=0, tiled=True)
    key_t = lax.dynamic_slice_in_dim(columns, kv_first * HD, kv_count * HD, 0)
    value_t = lax.dynamic_slice_in_dim(columns, (KV_HEADS + kv_first) * HD, kv_count * HD, 0)
    own_keys = prepare_keys(key_t.T, k_gain, position)
    own_values = value_t.T
    all_keys, all_values = (
        lax.all_gather(own_keys, "seq", axis=0, tiled=True),
        lax.all_gather(own_values, "seq", axis=0, tiled=True),
    )
    visible = key_pos[None, :] <= position[:, None]
    pieces = []
    for local in range(heads_here):
        query_cols = query_raw[:, local * HD : (local + 1) * HD]
        queries = (rotate(normalize(query_cols, q_gain), position) * HD ** (-0.5)).astype(
            jnp.bfloat16
        )
        scores = lax.dot_general(
            queries, all_keys, (((1,), (1,)), ((), ())), preferred_element_type=jnp.float32
        )
        scores = jnp.where(visible, scores, -jnp.inf)
        largest = jnp.max(scores, axis=-1, keepdims=True)
        expos = jnp.exp(scores - largest)
        probs = (expos / jnp.sum(expos, axis=-1, keepdims=True)).astype(jnp.bfloat16)
        pieces.append(
            jnp.dot(probs, all_values, preferred_element_type=jnp.float32).astype(jnp.bfloat16)
        )
    attended = jnp.concatenate(pieces, axis=-1)
    summed = lax.psum_scatter(
        jnp.dot(attended, w_out, preferred_element_type=jnp.float32).astype(jnp.bfloat16),
        "tensor",
        scatter_dimension=0,
        tiled=True,
    ).astype(jnp.float32)
    return (own_rows.astype(jnp.float32) + summed).astype(jnp.bfloat16)[None]


MESH = pl.DeviceIdType.MESH
Z = 4
X = 2


def layer_kernel(
    span_hbm, hidden_hbm, gain_hbm, q_gain_hbm, k_gain_hbm, wq_hbm, wkv_hbm, wo_hbm,
    out_ref,
    span_ref, hidden_ref, gain_ref, q_gain_ref, k_gain_ref, wkv_t_ref,
    rows_ref, wq_ref, wkv_ref, wo_ref, cos_ref, sin_ref, query_ref, kv_send, kv_in, key_own, key_other,
    value_other, part_ref, x_in, up_in, down_in, line_out,
    w_sem, row_recv, row_x_send, row_line_send, row_line_send2, kv_ssem, kv_rsem, pair_ssem, pair_rsem,
    x_ssem, x_rsem, line_ssem, up_rsem, down_rsem,
):
    t = lax.axis_index("tensor")
    s = lax.axis_index("seq")
    z = t // X
    x = t % X
    block = hidden_hbm.shape[1]
    half = block // 2
    chunk = X * block
    span_len = Z * chunk
    x_peer = z * X + (1 - x)
    low = z // 2
    far = z * low + (1 - low) * (3 - z)
    near = [far, 5 - far, 1, 0]
    order = [low * v + (1 - low) * (3 - v) for v in near]

    small_copies = [
        pltpu.make_async_copy(source, target, w_sem.at[3 + i])
        for i, (source, target) in enumerate([
            (hidden_hbm.at[0], hidden_ref), (gain_hbm, gain_ref), (span_hbm, span_ref),
            (q_gain_hbm, q_gain_ref), (k_gain_hbm, k_gain_ref),
        ])
    ]
    for copy in small_copies:
        copy.start()
    weight_copies = [
        pltpu.make_async_copy(wq_hbm, wq_ref, w_sem.at[0]),
        pltpu.make_async_copy(wkv_hbm, wkv_ref, w_sem.at[1]),
        pltpu.make_async_copy(wo_hbm, wo_ref, w_sem.at[2]),
    ]
    barrier = pltpu.get_barrier_semaphore()
    for step in range(1, Z * X):
        pl.semaphore_signal(
            barrier, inc=1, device_id={"tensor": (t + step) % (Z * X)}, device_id_type=MESH
        )
    pl.semaphore_signal(barrier, inc=1, device_id={"seq": 1 - s}, device_id_type=MESH)

    small_copies[0].wait()
    small_copies[1].wait()
    own = hidden_ref[...].astype(jnp.float32)
    scale = lax.rsqrt(jnp.mean(own * own, axis=-1, keepdims=True) + epsilon)
    own_start = pl.multiple_of(t * block, block)
    rows_ref[pl.ds(own_start, block), :] = (own * scale * gain_ref[...][None]).astype(jnp.bfloat16)
    pl.semaphore_wait(barrier, Z * X)

    def row_copy(zb, xb, h, target, send_sem):
        place = pl.ds(pl.multiple_of((zb * X + xb) * block + h * half, half), half)
        return pltpu.make_async_remote_copy(
            src_ref=rows_ref.at[place, :],
            dst_ref=rows_ref.at[place, :],
            send_sem=send_sem.at[zb, h],
            recv_sem=row_recv.at[zb * X + xb, h],
            device_id={"tensor": target},
            device_id_type=MESH,
        )

    def line_up(zb, h):
        return row_copy(zb, x, h, (t + X) % (Z * X), row_line_send)

    def line_down(zb, h):
        return row_copy(zb, x, h, (t + Z * X - X) % (Z * X), row_line_send2)

    def across(zb, h):
        return row_copy(zb, x, h, x_peer, row_x_send)

    def forward(zb, h):
        @pl.when((zb <= z) & (z < Z - 1))
        def _():
            line_up(zb, h).start()

        @pl.when((zb >= z) & (z > 0))
        def _():
            line_down(zb, h).start()

        across(zb, h).start()

    for h in range(2):
        forward(z, h)
    for copy in weight_copies:
        copy.start()
    for copy in small_copies[2:]:
        copy.wait()
    power = lax.broadcasted_iota(jnp.int32, (1, HD), 1) % (HD // 2)
    inverse = jnp.exp(power.astype(jnp.float32) * (-math.log(1000000.0) / (HD // 2)))
    position = span_ref[s] * span_len + lax.broadcasted_iota(jnp.int32, (span_len, HD), 0)
    angles = position.astype(jnp.float32) * inverse
    cos_ref[...] = jnp.cos(angles)
    lane = lax.broadcasted_iota(jnp.int32, (span_len, HD), 1)
    sine = jnp.sin(angles)
    sin_ref[...] = jnp.where(lane < HD // 2, -sine, sine)

    def norm_rotate(v, gain, zb):
        place = pl.ds(pl.multiple_of(zb * chunk, chunk), chunk)
        v = v * lax.rsqrt(jnp.mean(v * v, axis=-1, keepdims=True) + epsilon) * gain
        return v * cos_ref[place, :] + pltpu.roll(v, HD // 2, 1) * sin_ref[place, :]

    kind = t // Z

    def kv_copy(zb, j):
        return pltpu.make_async_remote_copy(
            src_ref=kv_send.at[zb, j],
            dst_ref=kv_in.at[kind, pl.ds(pl.multiple_of(zb * chunk, chunk), chunk), :],
            send_sem=kv_ssem.at[zb, j],
            recv_sem=kv_rsem.at[kind, zb],
            device_id={"tensor": (2 * t + j) % (Z * X)},
            device_id_type=MESH,
        )

    def project(zb):
        place = pl.ds(pl.multiple_of(zb * chunk, chunk), chunk)
        rows = rows_ref[place, :]
        kv = jnp.dot(rows, wkv_t_ref[...], preferred_element_type=jnp.float32).astype(jnp.bfloat16)
        for j in range(2):
            kv_send[zb, j] = kv[:, j * HD : (j + 1) * HD]
            here = (2 * t + j) % (Z * X) == t

            @pl.when(here)
            def _():
                kv_in[kind, place, :] = kv_send[zb, j]

            @pl.when(jnp.logical_not(here))
            def _():
                kv_copy(zb, j).start()

        raw = jnp.dot(rows, wq_ref[...], preferred_element_type=jnp.float32)
        for j in range(2):
            q = norm_rotate(raw[:, j * HD : (j + 1) * HD], q_gain_ref[...][None], zb) * HD ** (-0.5)
            query_ref[zb, j * chunk : (j + 1) * chunk, :] = q.astype(jnp.bfloat16)

    weight_copies[1].wait()
    wkv_t_ref[...] = wkv_ref[...].T
    weight_copies[0].wait()
    for k in range(1, Z):
        for h in range(2):
            row_copy(order[k], x, h, x_peer, row_x_send).wait_recv()
            forward(order[k], h)
        for done in ([], [0], [1, 2])[k - 1]:
            for h in range(2):
                row_copy(order[done], 1 - x, h, x_peer, row_x_send).wait_recv()
            project(order[done])
    for h in range(2):
        row_copy(order[Z - 1], 1 - x, h, x_peer, row_x_send).wait_recv()
    project(order[Z - 1])

    def pair_copy(index, zb, source, target):
        place = pl.ds(zb * chunk, chunk)
        return pltpu.make_async_remote_copy(
            src_ref=source.at[place, :],
            dst_ref=target.at[place, :],
            send_sem=pair_ssem.at[index, zb],
            recv_sem=pair_rsem.at[index, zb],
            device_id={"seq": 1 - s},
            device_id_type=MESH,
        )

    def kv_arrived(which, zb):
        @pl.when((t // 2 + which * Z) != t)
        def _():
            pltpu.make_async_remote_copy(
                src_ref=kv_send.at[zb, 0],
                dst_ref=kv_in.at[which, pl.ds(zb * chunk, chunk), :],
                send_sem=kv_ssem.at[zb, 0],
                recv_sem=kv_rsem.at[which, zb],
                device_id={"tensor": x_peer},
                device_id_type=MESH,
            ).wait_recv()

    values = kv_in.at[1]
    for zb in range(Z):
        kv_arrived(0, zb)
        place = slice(zb * chunk, (zb + 1) * chunk)
        raw = kv_in[0, place, :].astype(jnp.float32)
        key_own[place, :] = norm_rotate(raw, k_gain_ref[...][None], zb).astype(jnp.bfloat16)
        pair_copy(0, zb, key_own, key_other).start()
        kv_arrived(1, zb)
        pair_copy(1, zb, values, value_other).start()
    weight_copies[2].wait()
    for zb in range(Z):
        pair_copy(0, zb, key_own, key_other).wait_recv()
        pair_copy(1, zb, values, value_other).wait_recv()

    hide = jnp.where(span_ref[1 - s] < span_ref[s], 0.0, -1e30).astype(jnp.float32)

    def attend(zb):
        q = query_ref[zb]
        nt = (((1,), (1,)), ((), ()))
        mine = lax.dot_general(q, key_own[...], nt, preferred_element_type=jnp.float32)
        others = lax.dot_general(q, key_other[...], nt, preferred_element_type=jnp.float32) + hide
        row = lax.broadcasted_iota(jnp.int32, mine.shape, 0) % chunk + zb * chunk
        column = lax.broadcasted_iota(jnp.int32, mine.shape, 1)
        mine = jnp.where(column <= row, mine, -jnp.inf)
        largest = jnp.maximum(
            jnp.max(mine, axis=-1, keepdims=True), jnp.max(others, axis=-1, keepdims=True)
        )
        mine = jnp.exp(mine - largest)
        others = jnp.exp(others - largest)
        total = jnp.sum(mine, axis=-1, keepdims=True) + jnp.sum(others, axis=-1, keepdims=True)
        share = 1.0 / total
        result = jnp.dot(
            (mine * share).astype(jnp.bfloat16), kv_in[1], preferred_element_type=jnp.float32
        ) + jnp.dot(
            (others * share).astype(jnp.bfloat16), value_other[...], preferred_element_type=jnp.float32
        )
        result = result.astype(jnp.bfloat16)
        joined = jnp.concatenate([result[:chunk], result[chunk:]], axis=-1)
        part_ref[zb] = jnp.dot(joined, wo_ref[...], preferred_element_type=jnp.float32).astype(
            jnp.bfloat16
        )

    def part_copy(zb, h):
        place = pl.ds(pl.multiple_of((1 - x) * block + h * half, half), half)
        return pltpu.make_async_remote_copy(
            src_ref=part_ref.at[zb, place, :],
            dst_ref=x_in.at[zb, pl.ds(h * half, half), :],
            send_sem=x_ssem.at[zb, h],
            recv_sem=x_rsem.at[zb, h],
            device_id={"tensor": x_peer},
            device_id_type=MESH,
        )

    def sum_copy(zb, h, target_ref, recv_sem, target):
        place = pl.ds(h * half, half)
        return pltpu.make_async_remote_copy(
            src_ref=line_out.at[zb, place, :],
            dst_ref=target_ref.at[zb, place, :],
            send_sem=line_ssem.at[zb, h],
            recv_sem=recv_sem.at[zb, h],
            device_id={"tensor": target},
            device_id_type=MESH,
        )

    def sum_up(zb, h):
        return sum_copy(zb, h, up_in, up_rsem, (t + X) % (Z * X))

    def sum_down(zb, h):
        return sum_copy(zb, h, down_in, down_rsem, (t + Z * X - X) % (Z * X))

    back = order[::-1]
    for zb in back:
        attend(zb)
        for h in range(2):
            part_copy(zb, h).start()

    def pair_sum(zb, h):
        own_half = pl.ds(pl.multiple_of(x * block + h * half, half), half)
        mine = part_ref[zb, own_half, :].astype(jnp.float32)
        return mine + x_in[zb, h * half : (h + 1) * half, :].astype(jnp.float32)

    def combine(zb, h):
        place = slice(h * half, (h + 1) * half)
        part_copy(zb, h).wait_recv()

        @pl.when(zb > z)
        def _():
            @pl.when(z > 0)
            def _():
                sum_up(zb, h).wait_recv()
                line_out[zb, place, :] = (
                    pair_sum(zb, h) + up_in[zb, place, :].astype(jnp.float32)
                ).astype(jnp.bfloat16)

            @pl.when(z == 0)
            def _():
                line_out[zb, place, :] = pair_sum(zb, h).astype(jnp.bfloat16)

            sum_up(zb, h).start()

        @pl.when(zb < z)
        def _():
            @pl.when(z < Z - 1)
            def _():
                sum_down(zb, h).wait_recv()
                line_out[zb, place, :] = (
                    pair_sum(zb, h) + down_in[zb, place, :].astype(jnp.float32)
                ).astype(jnp.bfloat16)

            @pl.when(z == Z - 1)
            def _():
                line_out[zb, place, :] = pair_sum(zb, h).astype(jnp.bfloat16)

            sum_down(zb, h).start()

    for zb in back[: Z - 1]:
        for h in range(2):
            combine(zb, h)

    for h in range(2):
        place = slice(h * half, (h + 1) * half)
        part_copy(z, h).wait_recv()
        total = hidden_ref[place, :].astype(jnp.float32) + pair_sum(z, h)

        @pl.when(z == 0)
        def _():
            sum_down(z, h).wait_recv()
            out_ref[place, :] = (total + down_in[z, place, :].astype(jnp.float32)).astype(jnp.bfloat16)

        @pl.when(z == Z - 1)
        def _():
            sum_up(z, h).wait_recv()
            out_ref[place, :] = (total + up_in[z, place, :].astype(jnp.float32)).astype(jnp.bfloat16)

        @pl.when((z > 0) & (z < Z - 1))
        def _():
            sum_down(z, h).wait_recv()
            sum_up(z, h).wait_recv()
            out_ref[place, :] = (
                total + down_in[z, place, :].astype(jnp.float32) + up_in[z, place, :].astype(jnp.float32)
            ).astype(jnp.bfloat16)

    for zb in range(Z):
        for h in range(2):
            across(zb, h).wait_send()
            part_copy(zb, h).wait_send()

            @pl.when((zb <= z) & (z < Z - 1))
            def _():
                line_up(zb, h).wait_send()

            @pl.when((zb >= z) & (z > 0))
            def _():
                line_down(zb, h).wait_send()

            @pl.when(zb != z)
            def _():
                sum_up(zb, h).wait_send()

        pair_copy(0, zb, key_own, key_other).wait_send()
        pair_copy(1, zb, values, value_other).wait_send()
        for j in range(2):
            @pl.when((2 * t + j) % (Z * X) != t)
            def _():
                kv_copy(zb, j).wait_send()


def fused_body(hidden_in, span_order, norm_gain, w_query, w_keyval_t, q_gain, k_gain, w_out):
    _, block, width = hidden_in.shape
    chunk = X * block
    span_len = Z * chunk
    vmem = pl.BlockSpec(memory_space=pltpu.VMEM)
    hbm = pl.BlockSpec(memory_space=pltpu.HBM)
    bf16 = jnp.bfloat16
    dma = pltpu.SemaphoreType.DMA
    out = pl.pallas_call(
        layer_kernel,
        out_shape=jax.ShapeDtypeStruct((block, width), bf16),
        in_specs=[hbm] * 8,
        out_specs=vmem,
        scratch_shapes=[
            pltpu.SMEM(span_order.shape, jnp.int32),
            pltpu.VMEM((block, width), bf16),
            pltpu.VMEM(norm_gain.shape, jnp.float32),
            pltpu.VMEM(q_gain.shape, jnp.float32),
            pltpu.VMEM(k_gain.shape, jnp.float32),
            pltpu.VMEM((width, w_keyval_t.shape[0]), bf16),
            pltpu.VMEM((span_len, width), bf16),
            pltpu.VMEM(w_query.shape, bf16),
            pltpu.VMEM(w_keyval_t.shape, bf16),
            pltpu.VMEM(w_out.shape, bf16),
            pltpu.VMEM((span_len, HD), jnp.float32),
            pltpu.VMEM((span_len, HD), jnp.float32),
            pltpu.VMEM((Z, 2 * chunk, HD), bf16),
            pltpu.VMEM((Z, 2, chunk, HD), bf16),
            pltpu.VMEM((2, span_len, HD), bf16),
            pltpu.VMEM((span_len, HD), bf16),
            pltpu.VMEM((span_len, HD), bf16),
            pltpu.VMEM((span_len, HD), bf16),
            pltpu.VMEM((Z, chunk, width), bf16),
            pltpu.VMEM((Z, block, width), bf16),
            pltpu.VMEM((Z, block, width), bf16),
            pltpu.VMEM((Z, block, width), bf16),
            pltpu.VMEM((Z, block, width), bf16),
            dma((8,)),
            dma((Z * X, 2)),
            dma((Z, 2)),
            dma((Z, 2)),
            dma((Z, 2)),
            dma((Z, 2)),
            dma((2, Z)),
            dma((2, Z)),
            dma((2, Z)),
            dma((Z, 2)),
            dma((Z, 2)),
            dma((Z, 2)),
            dma((Z, 2)),
            dma((Z, 2)),
        ],
        compiler_params=pltpu.CompilerParams(
            collective_id=0, has_side_effects=True, vmem_limit_bytes=64 * 1024 * 1024
        ),
    )(
        span_order, hidden_in, norm_gain, q_gain, k_gain,
        w_query, w_keyval_t, w_out,
    )
    return out[None]


def solution(mesh):
    placed = (
        P(("groups", "seq"), "tensor", None),
        P("groups"),
        P(),
        P(None, "tensor"),
        P("tensor", None),
        P(),
        P(),
        P("tensor", None),
    )
    def chosen(hidden_in, span_order, norm_gain, w_query, *rest):
        fits = (
            mesh.shape["tensor"] == Z * X
            and mesh.shape["seq"] == 2
            and w_query.shape[1] == 2 * HD
            and hidden_in.shape[1] % 32 == 0
        )
        run = fused_body if fits else body
        return run(hidden_in, span_order, norm_gain, w_query, *rest)

    return jax.shard_map(
        chosen,
        mesh=mesh,
        in_specs=placed,
        out_specs=P(("groups", "seq"), "tensor", None),
        check_vma=False,
    )
```

```python
import math
import jax
import jax.numpy as jnp
from jax import lax
from jax.experimental import pallas as pl
from jax.experimental.pallas import tpu as pltpu
from jax.sharding import PartitionSpec as P

HD = 128
KV_HEADS = 8


epsilon = 1e-06


def normalize(vector, gain):
    vector = vector.astype(jnp.float32)
    return vector * lax.rsqrt(jnp.mean(vector * vector, axis=-1, keepdims=True) + epsilon) * gain


def rotate(vector, position):
    half_dim = vector.shape[-1] // 2
    inverse = 1000000.0 ** (-2.0 * jnp.arange(half_dim, dtype=jnp.float32) / vector.shape[-1])
    angles = position.astype(jnp.float32)[:, None] * inverse[None, :]
    cosine = jnp.cos(angles)
    sine = jnp.sin(angles)
    front = vector[:, :half_dim]
    back = vector[:, half_dim:]
    return jnp.concatenate([front * cosine - back * sine, back * cosine + front * sine], axis=-1)


def prepare_keys(key_rows, gain, position):
    blocks = rotate(normalize(key_rows, gain), position)
    return blocks.astype(jnp.bfloat16)


def body(hidden_in, span_order, norm_gain, w_query, w_keyval_t, q_gain, k_gain, w_out):
    own_rows = hidden_in[0]
    rows_here = own_rows.shape[0]
    tensor_size = lax.axis_size("tensor")
    seq_size = lax.axis_size("seq")
    span_len = rows_here * tensor_size
    heads_here = w_query.shape[1] // HD
    group_size = heads_here * tensor_size // KV_HEADS
    kv_count = max(1, heads_here // group_size)
    own_normed = normalize(own_rows, norm_gain).astype(jnp.bfloat16)
    gathered = lax.all_gather(own_normed, "tensor", axis=0, tiled=True)
    slot_index = lax.axis_index("seq")
    offsets = jnp.arange(span_len, dtype=jnp.int32)
    position = span_order[slot_index] * span_len + offsets
    key_pos = (span_order[:, None] * span_len + offsets[None, :]).reshape(seq_size * span_len)
    query_raw = jnp.dot(gathered, w_query, preferred_element_type=jnp.float32)
    kv_columns = lax.dot_general(
        w_keyval_t, gathered, (((1,), (1,)), ((), ())), preferred_element_type=jnp.float32
    ).astype(jnp.bfloat16)
    kv_first = lax.axis_index("tensor") * heads_here // group_size
    columns = lax.all_gather(kv_columns, "tensor", axis=0, tiled=True)
    key_t = lax.dynamic_slice_in_dim(columns, kv_first * HD, kv_count * HD, 0)
    value_t = lax.dynamic_slice_in_dim(columns, (KV_HEADS + kv_first) * HD, kv_count * HD, 0)
    own_keys = prepare_keys(key_t.T, k_gain, position)
    own_values = value_t.T
    all_keys, all_values = (
        lax.all_gather(own_keys, "seq", axis=0, tiled=True),
        lax.all_gather(own_values, "seq", axis=0, tiled=True),
    )
    visible = key_pos[None, :] <= position[:, None]
    pieces = []
    for local in range(heads_here):
        query_cols = query_raw[:, local * HD : (local + 1) * HD]
        queries = (rotate(normalize(query_cols, q_gain), position) * HD ** (-0.5)).astype(
            jnp.bfloat16
        )
        scores = lax.dot_general(
            queries, all_keys, (((1,), (1,)), ((), ())), preferred_element_type=jnp.float32
        )
        scores = jnp.where(visible, scores, -jnp.inf)
        largest = jnp.max(scores, axis=-1, keepdims=True)
        expos = jnp.exp(scores - largest)
        probs = (expos / jnp.sum(expos, axis=-1, keepdims=True)).astype(jnp.bfloat16)
        pieces.append(
            jnp.dot(probs, all_values, preferred_element_type=jnp.float32).astype(jnp.bfloat16)
        )
    attended = jnp.concatenate(pieces, axis=-1)
    summed = lax.psum_scatter(
        jnp.dot(attended, w_out, preferred_element_type=jnp.float32).astype(jnp.bfloat16),
        "tensor",
        scatter_dimension=0,
        tiled=True,
    ).astype(jnp.float32)
    return (own_rows.astype(jnp.float32) + summed).astype(jnp.bfloat16)[None]


MESH = pl.DeviceIdType.MESH
Z = 4
X = 2
PIECES = 4


def layer_kernel(
    span_hbm, hidden_hbm, gain_hbm, q_gain_hbm, k_gain_hbm, wq_hbm, wkv_hbm, wo_hbm,
    out_ref,
    span_ref, hidden_ref, gain_ref, q_gain_ref, k_gain_ref, wkv_t_ref,
    rows_ref, wq_ref, wkv_ref, wo_ref, cos_ref, sin_ref, query_ref, kv_send, kv_in, key_own, key_other,
    value_other, part_ref, x_in, up_in, down_in, line_out,
    w_sem, row_recv, row_x_send, row_line_send, row_line_send2, kv_ssem, kv_rsem, pair_ssem, pair_rsem,
    x_ssem, x_rsem, line_ssem, up_rsem, down_rsem,
):
    t = lax.axis_index("tensor")
    s = lax.axis_index("seq")
    z = t // X
    x = t % X
    block = hidden_hbm.shape[1]
    piece = block // PIECES
    chunk = X * block
    span_len = Z * chunk
    x_peer = z * X + (1 - x)
    low = z // 2
    far = z * low + (1 - low) * (3 - z)
    near = [far, 5 - far, 1, 0]
    order = [low * v + (1 - low) * (3 - v) for v in near]

    small_copies = [
        pltpu.make_async_copy(source, target, w_sem.at[3 + i])
        for i, (source, target) in enumerate([
            (hidden_hbm.at[0], hidden_ref), (gain_hbm, gain_ref), (span_hbm, span_ref),
            (q_gain_hbm, q_gain_ref), (k_gain_hbm, k_gain_ref),
        ])
    ]
    for copy in small_copies:
        copy.start()
    weight_copies = [
        pltpu.make_async_copy(wq_hbm, wq_ref, w_sem.at[0]),
        pltpu.make_async_copy(wkv_hbm, wkv_ref, w_sem.at[1]),
        pltpu.make_async_copy(wo_hbm, wo_ref, w_sem.at[2]),
    ]
    barrier = pltpu.get_barrier_semaphore()
    for step in range(1, Z * X):
        pl.semaphore_signal(
            barrier, inc=1, device_id={"tensor": (t + step) % (Z * X)}, device_id_type=MESH
        )
    pl.semaphore_signal(barrier, inc=1, device_id={"seq": 1 - s}, device_id_type=MESH)

    small_copies[0].wait()
    small_copies[1].wait()
    own = hidden_ref[...].astype(jnp.float32)
    scale = lax.rsqrt(jnp.mean(own * own, axis=-1, keepdims=True) + epsilon)
    own_start = pl.multiple_of(t * block, block)
    rows_ref[pl.ds(own_start, block), :] = (own * scale * gain_ref[...][None]).astype(jnp.bfloat16)
    pl.semaphore_wait(barrier, Z * X)

    def row_copy(zb, xb, h, target, send_sem):
        place = pl.ds(pl.multiple_of((zb * X + xb) * block + h * piece, piece), piece)
        return pltpu.make_async_remote_copy(
            src_ref=rows_ref.at[place, :],
            dst_ref=rows_ref.at[place, :],
            send_sem=send_sem.at[zb, h],
            recv_sem=row_recv.at[zb * X + xb, h],
            device_id={"tensor": target},
            device_id_type=MESH,
        )

    def line_up(zb, h):
        return row_copy(zb, x, h, (t + X) % (Z * X), row_line_send)

    def line_down(zb, h):
        return row_copy(zb, x, h, (t + Z * X - X) % (Z * X), row_line_send2)

    def across(zb, h):
        return row_copy(zb, x, h, x_peer, row_x_send)

    def forward(zb, h):
        @pl.when((zb <= z) & (z < Z - 1))
        def _():
            line_up(zb, h).start()

        @pl.when((zb >= z) & (z > 0))
        def _():
            line_down(zb, h).start()

        across(zb, h).start()

    for h in range(PIECES):
        forward(z, h)
    for copy in weight_copies:
        copy.start()
    for copy in small_copies[2:]:
        copy.wait()
    power = lax.broadcasted_iota(jnp.int32, (1, HD), 1) % (HD // 2)
    inverse = jnp.exp(power.astype(jnp.float32) * (-math.log(1000000.0) / (HD // 2)))
    position = span_ref[s] * span_len + lax.broadcasted_iota(jnp.int32, (span_len, HD), 0)
    angles = position.astype(jnp.float32) * inverse
    cos_ref[...] = jnp.cos(angles)
    lane = lax.broadcasted_iota(jnp.int32, (span_len, HD), 1)
    sine = jnp.sin(angles)
    sin_ref[...] = jnp.where(lane < HD // 2, -sine, sine)

    def norm_rotate(v, gain, zb):
        place = pl.ds(pl.multiple_of(zb * chunk, chunk), chunk)
        v = v * lax.rsqrt(jnp.mean(v * v, axis=-1, keepdims=True) + epsilon) * gain
        return v * cos_ref[place, :] + pltpu.roll(v, HD // 2, 1) * sin_ref[place, :]

    kind = t // Z

    def kv_copy(zb, j):
        return pltpu.make_async_remote_copy(
            src_ref=kv_send.at[zb, j],
            dst_ref=kv_in.at[kind, pl.ds(pl.multiple_of(zb * chunk, chunk), chunk), :],
            send_sem=kv_ssem.at[zb, j],
            recv_sem=kv_rsem.at[kind, zb],
            device_id={"tensor": (2 * t + j) % (Z * X)},
            device_id_type=MESH,
        )

    def project(zb):
        place = pl.ds(pl.multiple_of(zb * chunk, chunk), chunk)
        rows = rows_ref[place, :]
        kv = jnp.dot(rows, wkv_t_ref[...], preferred_element_type=jnp.float32).astype(jnp.bfloat16)
        for j in range(2):
            kv_send[zb, j] = kv[:, j * HD : (j + 1) * HD]
            here = (2 * t + j) % (Z * X) == t

            @pl.when(here)
            def _():
                kv_in[kind, place, :] = kv_send[zb, j]

            @pl.when(jnp.logical_not(here))
            def _():
                kv_copy(zb, j).start()

        raw = jnp.dot(rows, wq_ref[...], preferred_element_type=jnp.float32)
        for j in range(2):
            q = norm_rotate(raw[:, j * HD : (j + 1) * HD], q_gain_ref[...][None], zb) * HD ** (-0.5)
            query_ref[zb, j * chunk : (j + 1) * chunk, :] = q.astype(jnp.bfloat16)

    weight_copies[1].wait()
    wkv_t_ref[...] = wkv_ref[...].T
    weight_copies[0].wait()
    for k in range(1, Z):
        for h in range(PIECES):
            row_copy(order[k], x, h, x_peer, row_x_send).wait_recv()
            forward(order[k], h)
        for done in ([], [0], [1, 2])[k - 1]:
            for h in range(PIECES):
                row_copy(order[done], 1 - x, h, x_peer, row_x_send).wait_recv()
            project(order[done])
    for h in range(PIECES):
        row_copy(order[Z - 1], 1 - x, h, x_peer, row_x_send).wait_recv()
    project(order[Z - 1])

    def pair_copy(index, zb, source, target):
        place = pl.ds(zb * chunk, chunk)
        return pltpu.make_async_remote_copy(
            src_ref=source.at[place, :],
            dst_ref=target.at[place, :],
            send_sem=pair_ssem.at[index, zb],
            recv_sem=pair_rsem.at[index, zb],
            device_id={"seq": 1 - s},
            device_id_type=MESH,
        )

    def kv_arrived(which, zb):
        @pl.when((t // 2 + which * Z) != t)
        def _():
            pltpu.make_async_remote_copy(
                src_ref=kv_send.at[zb, 0],
                dst_ref=kv_in.at[which, pl.ds(zb * chunk, chunk), :],
                send_sem=kv_ssem.at[zb, 0],
                recv_sem=kv_rsem.at[which, zb],
                device_id={"tensor": x_peer},
                device_id_type=MESH,
            ).wait_recv()

    values = kv_in.at[1]
    for zb in range(Z):
        kv_arrived(0, zb)
        place = slice(zb * chunk, (zb + 1) * chunk)
        raw = kv_in[0, place, :].astype(jnp.float32)
        key_own[place, :] = norm_rotate(raw, k_gain_ref[...][None], zb).astype(jnp.bfloat16)
        pair_copy(0, zb, key_own, key_other).start()
        kv_arrived(1, zb)
        pair_copy(1, zb, values, value_other).start()
    weight_copies[2].wait()
    for zb in range(Z):
        pair_copy(0, zb, key_own, key_other).wait_recv()
        pair_copy(1, zb, values, value_other).wait_recv()

    hide = jnp.where(span_ref[1 - s] < span_ref[s], 0.0, -1e30).astype(jnp.float32)

    def attend(zb):
        q = query_ref[zb]
        nt = (((1,), (1,)), ((), ()))
        mine = lax.dot_general(q, key_own[...], nt, preferred_element_type=jnp.float32)
        others = lax.dot_general(q, key_other[...], nt, preferred_element_type=jnp.float32) + hide
        row = lax.broadcasted_iota(jnp.int32, mine.shape, 0) % chunk + zb * chunk
        column = lax.broadcasted_iota(jnp.int32, mine.shape, 1)
        mine = jnp.where(column <= row, mine, -jnp.inf)
        largest = jnp.maximum(
            jnp.max(mine, axis=-1, keepdims=True), jnp.max(others, axis=-1, keepdims=True)
        )
        mine = jnp.exp(mine - largest)
        others = jnp.exp(others - largest)
        total = jnp.sum(mine, axis=-1, keepdims=True) + jnp.sum(others, axis=-1, keepdims=True)
        share = 1.0 / total
        result = jnp.dot(
            (mine * share).astype(jnp.bfloat16), kv_in[1], preferred_element_type=jnp.float32
        ) + jnp.dot(
            (others * share).astype(jnp.bfloat16), value_other[...], preferred_element_type=jnp.float32
        )
        result = result.astype(jnp.bfloat16)
        joined = jnp.concatenate([result[:chunk], result[chunk:]], axis=-1)
        part_ref[zb] = jnp.dot(joined, wo_ref[...], preferred_element_type=jnp.float32).astype(
            jnp.bfloat16
        )

    def part_copy(zb, h):
        place = pl.ds(pl.multiple_of((1 - x) * block + h * piece, piece), piece)
        return pltpu.make_async_remote_copy(
            src_ref=part_ref.at[zb, place, :],
            dst_ref=x_in.at[zb, pl.ds(h * piece, piece), :],
            send_sem=x_ssem.at[zb, h],
            recv_sem=x_rsem.at[zb, h],
            device_id={"tensor": x_peer},
            device_id_type=MESH,
        )

    def sum_copy(zb, h, target_ref, recv_sem, target):
        place = pl.ds(h * piece, piece)
        return pltpu.make_async_remote_copy(
            src_ref=line_out.at[zb, place, :],
            dst_ref=target_ref.at[zb, place, :],
            send_sem=line_ssem.at[zb, h],
            recv_sem=recv_sem.at[zb, h],
            device_id={"tensor": target},
            device_id_type=MESH,
        )

    def sum_up(zb, h):
        return sum_copy(zb, h, up_in, up_rsem, (t + X) % (Z * X))

    def sum_down(zb, h):
        return sum_copy(zb, h, down_in, down_rsem, (t + Z * X - X) % (Z * X))

    back = order[::-1]
    for zb in back:
        attend(zb)
        for h in range(PIECES):
            part_copy(zb, h).start()

    def pair_sum(zb, h):
        own_half = pl.ds(pl.multiple_of(x * block + h * piece, piece), piece)
        mine = part_ref[zb, own_half, :].astype(jnp.float32)
        return mine + x_in[zb, h * piece : (h + 1) * piece, :].astype(jnp.float32)

    def combine(zb, h):
        place = slice(h * piece, (h + 1) * piece)
        part_copy(zb, h).wait_recv()

        @pl.when(zb > z)
        def _():
            @pl.when(z > 0)
            def _():
                sum_up(zb, h).wait_recv()
                line_out[zb, place, :] = (
                    pair_sum(zb, h) + up_in[zb, place, :].astype(jnp.float32)
                ).astype(jnp.bfloat16)

            @pl.when(z == 0)
            def _():
                line_out[zb, place, :] = pair_sum(zb, h).astype(jnp.bfloat16)

            sum_up(zb, h).start()

        @pl.when(zb < z)
        def _():
            @pl.when(z < Z - 1)
            def _():
                sum_down(zb, h).wait_recv()
                line_out[zb, place, :] = (
                    pair_sum(zb, h) + down_in[zb, place, :].astype(jnp.float32)
                ).astype(jnp.bfloat16)

            @pl.when(z == Z - 1)
            def _():
                line_out[zb, place, :] = pair_sum(zb, h).astype(jnp.bfloat16)

            sum_down(zb, h).start()

    for zb in back[: Z - 1]:
        for h in range(PIECES):
            combine(zb, h)

    for h in range(PIECES):
        place = slice(h * piece, (h + 1) * piece)
        part_copy(z, h).wait_recv()
        total = hidden_ref[place, :].astype(jnp.float32) + pair_sum(z, h)

        @pl.when(z == 0)
        def _():
            sum_down(z, h).wait_recv()
            out_ref[place, :] = (total + down_in[z, place, :].astype(jnp.float32)).astype(jnp.bfloat16)

        @pl.when(z == Z - 1)
        def _():
            sum_up(z, h).wait_recv()
            out_ref[place, :] = (total + up_in[z, place, :].astype(jnp.float32)).astype(jnp.bfloat16)

        @pl.when((z > 0) & (z < Z - 1))
        def _():
            sum_down(z, h).wait_recv()
            sum_up(z, h).wait_recv()
            out_ref[place, :] = (
                total + down_in[z, place, :].astype(jnp.float32) + up_in[z, place, :].astype(jnp.float32)
            ).astype(jnp.bfloat16)

    for zb in range(Z):
        for h in range(PIECES):
            across(zb, h).wait_send()
            part_copy(zb, h).wait_send()

            @pl.when((zb <= z) & (z < Z - 1))
            def _():
                line_up(zb, h).wait_send()

            @pl.when((zb >= z) & (z > 0))
            def _():
                line_down(zb, h).wait_send()

            @pl.when(zb != z)
            def _():
                sum_up(zb, h).wait_send()

        pair_copy(0, zb, key_own, key_other).wait_send()
        pair_copy(1, zb, values, value_other).wait_send()
        for j in range(2):
            @pl.when((2 * t + j) % (Z * X) != t)
            def _():
                kv_copy(zb, j).wait_send()


def fused_body(hidden_in, span_order, norm_gain, w_query, w_keyval_t, q_gain, k_gain, w_out):
    _, block, width = hidden_in.shape
    chunk = X * block
    span_len = Z * chunk
    vmem = pl.BlockSpec(memory_space=pltpu.VMEM)
    hbm = pl.BlockSpec(memory_space=pltpu.HBM)
    bf16 = jnp.bfloat16
    dma = pltpu.SemaphoreType.DMA
    out = pl.pallas_call(
        layer_kernel,
        out_shape=jax.ShapeDtypeStruct((block, width), bf16),
        in_specs=[hbm] * 8,
        out_specs=vmem,
        scratch_shapes=[
            pltpu.SMEM(span_order.shape, jnp.int32),
            pltpu.VMEM((block, width), bf16),
            pltpu.VMEM(norm_gain.shape, jnp.float32),
            pltpu.VMEM(q_gain.shape, jnp.float32),
            pltpu.VMEM(k_gain.shape, jnp.float32),
            pltpu.VMEM((width, w_keyval_t.shape[0]), bf16),
            pltpu.VMEM((span_len, width), bf16),
            pltpu.VMEM(w_query.shape, bf16),
            pltpu.VMEM(w_keyval_t.shape, bf16),
            pltpu.VMEM(w_out.shape, bf16),
            pltpu.VMEM((span_len, HD), jnp.float32),
            pltpu.VMEM((span_len, HD), jnp.float32),
            pltpu.VMEM((Z, 2 * chunk, HD), bf16),
            pltpu.VMEM((Z, 2, chunk, HD), bf16),
            pltpu.VMEM((2, span_len, HD), bf16),
            pltpu.VMEM((span_len, HD), bf16),
            pltpu.VMEM((span_len, HD), bf16),
            pltpu.VMEM((span_len, HD), bf16),
            pltpu.VMEM((Z, chunk, width), bf16),
            pltpu.VMEM((Z, block, width), bf16),
            pltpu.VMEM((Z, block, width), bf16),
            pltpu.VMEM((Z, block, width), bf16),
            pltpu.VMEM((Z, block, width), bf16),
            dma((8,)),
            dma((Z * X, PIECES)),
            dma((Z, PIECES)),
            dma((Z, PIECES)),
            dma((Z, PIECES)),
            dma((Z, PIECES)),
            dma((2, Z)),
            dma((2, Z)),
            dma((2, Z)),
            dma((Z, PIECES)),
            dma((Z, PIECES)),
            dma((Z, PIECES)),
            dma((Z, PIECES)),
            dma((Z, PIECES)),
        ],
        compiler_params=pltpu.CompilerParams(
            collective_id=0, has_side_effects=True, vmem_limit_bytes=64 * 1024 * 1024
        ),
    )(
        span_order, hidden_in, norm_gain, q_gain, k_gain,
        w_query, w_keyval_t, w_out,
    )
    return out[None]


def solution(mesh):
    placed = (
        P(("groups", "seq"), "tensor", None),
        P("groups"),
        P(),
        P(None, "tensor"),
        P("tensor", None),
        P(),
        P(),
        P("tensor", None),
    )
    def chosen(hidden_in, span_order, norm_gain, w_query, *rest):
        fits = (
            mesh.shape["tensor"] == Z * X
            and mesh.shape["seq"] == 2
            and w_query.shape[1] == 2 * HD
            and hidden_in.shape[1] % (16 * PIECES) == 0
        )
        run = fused_body if fits else body
        return run(hidden_in, span_order, norm_gain, w_query, *rest)

    return jax.shard_map(
        chosen,
        mesh=mesh,
        in_specs=placed,
        out_specs=P(("groups", "seq"), "tensor", None),
        check_vma=False,
    )
```

```python
import math
import jax
import jax.numpy as jnp
from jax import lax
from jax.experimental import pallas as pl
from jax.experimental.pallas import tpu as pltpu
from jax.sharding import PartitionSpec as P

HD = 128
KV_HEADS = 8


epsilon = 1e-06


def normalize(vector, gain):
    vector = vector.astype(jnp.float32)
    return vector * lax.rsqrt(jnp.mean(vector * vector, axis=-1, keepdims=True) + epsilon) * gain


def rotate(vector, position):
    half_dim = vector.shape[-1] // 2
    inverse = 1000000.0 ** (-2.0 * jnp.arange(half_dim, dtype=jnp.float32) / vector.shape[-1])
    angles = position.astype(jnp.float32)[:, None] * inverse[None, :]
    cosine = jnp.cos(angles)
    sine = jnp.sin(angles)
    front = vector[:, :half_dim]
    back = vector[:, half_dim:]
    return jnp.concatenate([front * cosine - back * sine, back * cosine + front * sine], axis=-1)


def prepare_keys(key_rows, gain, position):
    blocks = rotate(normalize(key_rows, gain), position)
    return blocks.astype(jnp.bfloat16)


def body(hidden_in, span_order, norm_gain, w_query, w_keyval_t, q_gain, k_gain, w_out):
    own_rows = hidden_in[0]
    rows_here = own_rows.shape[0]
    tensor_size = lax.axis_size("tensor")
    seq_size = lax.axis_size("seq")
    span_len = rows_here * tensor_size
    heads_here = w_query.shape[1] // HD
    group_size = heads_here * tensor_size // KV_HEADS
    kv_count = max(1, heads_here // group_size)
    own_normed = normalize(own_rows, norm_gain).astype(jnp.bfloat16)
    gathered = lax.all_gather(own_normed, "tensor", axis=0, tiled=True)
    slot_index = lax.axis_index("seq")
    offsets = jnp.arange(span_len, dtype=jnp.int32)
    position = span_order[slot_index] * span_len + offsets
    key_pos = (span_order[:, None] * span_len + offsets[None, :]).reshape(seq_size * span_len)
    query_raw = jnp.dot(gathered, w_query, preferred_element_type=jnp.float32)
    kv_columns = lax.dot_general(
        w_keyval_t, gathered, (((1,), (1,)), ((), ())), preferred_element_type=jnp.float32
    ).astype(jnp.bfloat16)
    kv_first = lax.axis_index("tensor") * heads_here // group_size
    columns = lax.all_gather(kv_columns, "tensor", axis=0, tiled=True)
    key_t = lax.dynamic_slice_in_dim(columns, kv_first * HD, kv_count * HD, 0)
    value_t = lax.dynamic_slice_in_dim(columns, (KV_HEADS + kv_first) * HD, kv_count * HD, 0)
    own_keys = prepare_keys(key_t.T, k_gain, position)
    own_values = value_t.T
    all_keys, all_values = (
        lax.all_gather(own_keys, "seq", axis=0, tiled=True),
        lax.all_gather(own_values, "seq", axis=0, tiled=True),
    )
    visible = key_pos[None, :] <= position[:, None]
    pieces = []
    for local in range(heads_here):
        query_cols = query_raw[:, local * HD : (local + 1) * HD]
        queries = (rotate(normalize(query_cols, q_gain), position) * HD ** (-0.5)).astype(
            jnp.bfloat16
        )
        scores = lax.dot_general(
            queries, all_keys, (((1,), (1,)), ((), ())), preferred_element_type=jnp.float32
        )
        scores = jnp.where(visible, scores, -jnp.inf)
        largest = jnp.max(scores, axis=-1, keepdims=True)
        expos = jnp.exp(scores - largest)
        probs = (expos / jnp.sum(expos, axis=-1, keepdims=True)).astype(jnp.bfloat16)
        pieces.append(
            jnp.dot(probs, all_values, preferred_element_type=jnp.float32).astype(jnp.bfloat16)
        )
    attended = jnp.concatenate(pieces, axis=-1)
    summed = lax.psum_scatter(
        jnp.dot(attended, w_out, preferred_element_type=jnp.float32).astype(jnp.bfloat16),
        "tensor",
        scatter_dimension=0,
        tiled=True,
    ).astype(jnp.float32)
    return (own_rows.astype(jnp.float32) + summed).astype(jnp.bfloat16)[None]


MESH = pl.DeviceIdType.MESH
Z = 4
X = 2
PIECES = 4


def layer_kernel(
    span_hbm, hidden_hbm, gain_hbm, q_gain_hbm, k_gain_hbm, wq_hbm, wkv_hbm, wo_hbm,
    out_ref,
    span_ref, hidden_ref, gain_ref, q_gain_ref, k_gain_ref, wkv_t_ref,
    rows_ref, wq_ref, wkv_ref, wo_ref, cos_ref, sin_ref, query_ref, kv_send, kv_in, key_own, key_other,
    value_other, part_ref, x_in, up_in, down_in, line_out,
    w_sem, row_recv, row_x_send, row_line_send, row_line_send2, kv_ssem, kv_rsem, pair_ssem, pair_rsem,
    x_ssem, x_rsem, line_ssem, up_rsem, down_rsem,
):
    t = lax.axis_index("tensor")
    s = lax.axis_index("seq")
    z = t // X
    x = t % X
    block = hidden_hbm.shape[1]
    piece = block // PIECES
    chunk = X * block
    span_len = Z * chunk
    x_peer = z * X + (1 - x)
    low = z // 2
    far = z * low + (1 - low) * (3 - z)
    near = [far, 5 - far, 1, 0]
    order = [low * v + (1 - low) * (3 - v) for v in near]

    small_copies = [
        pltpu.make_async_copy(source, target, w_sem.at[3 + i])
        for i, (source, target) in enumerate([
            (hidden_hbm.at[0], hidden_ref), (gain_hbm, gain_ref), (span_hbm, span_ref),
            (q_gain_hbm, q_gain_ref), (k_gain_hbm, k_gain_ref),
        ])
    ]
    for copy in small_copies:
        copy.start()
    weight_copies = [
        pltpu.make_async_copy(wq_hbm, wq_ref, w_sem.at[0]),
        pltpu.make_async_copy(wkv_hbm, wkv_ref, w_sem.at[1]),
        pltpu.make_async_copy(wo_hbm, wo_ref, w_sem.at[2]),
    ]
    barrier = pltpu.get_barrier_semaphore()
    for step in range(1, Z * X):
        pl.semaphore_signal(
            barrier, inc=1, device_id={"tensor": (t + step) % (Z * X)}, device_id_type=MESH
        )
    pl.semaphore_signal(barrier, inc=1, device_id={"seq": 1 - s}, device_id_type=MESH)

    small_copies[0].wait()
    small_copies[1].wait()
    own = hidden_ref[...].astype(jnp.float32)
    scale = lax.rsqrt(jnp.mean(own * own, axis=-1, keepdims=True) + epsilon)
    own_start = pl.multiple_of(t * block, block)
    rows_ref[pl.ds(own_start, block), :] = (own * scale * gain_ref[...][None]).astype(jnp.bfloat16)
    pl.semaphore_wait(barrier, Z * X)

    def row_copy(zb, xb, h, target, send_sem):
        place = pl.ds(pl.multiple_of((zb * X + xb) * block + h * piece, piece), piece)
        return pltpu.make_async_remote_copy(
            src_ref=rows_ref.at[place, :],
            dst_ref=rows_ref.at[place, :],
            send_sem=send_sem.at[zb, h],
            recv_sem=row_recv.at[zb * X + xb, h],
            device_id={"tensor": target},
            device_id_type=MESH,
        )

    def line_up(zb, h):
        return row_copy(zb, x, h, (t + X) % (Z * X), row_line_send)

    def line_down(zb, h):
        return row_copy(zb, x, h, (t + Z * X - X) % (Z * X), row_line_send2)

    def across(zb, h):
        return row_copy(zb, x, h, x_peer, row_x_send)

    def forward(zb, h):
        @pl.when((zb <= z) & (z < Z - 1))
        def _():
            line_up(zb, h).start()

        @pl.when((zb >= z) & (z > 0))
        def _():
            line_down(zb, h).start()

        across(zb, h).start()

    for h in range(PIECES):
        forward(z, h)
    for copy in weight_copies:
        copy.start()
    for copy in small_copies[2:]:
        copy.wait()
    power = lax.broadcasted_iota(jnp.int32, (1, HD), 1) % (HD // 2)
    inverse = jnp.exp(power.astype(jnp.float32) * (-math.log(1000000.0) / (HD // 2)))
    position = span_ref[s] * span_len + lax.broadcasted_iota(jnp.int32, (span_len, HD), 0)
    angles = position.astype(jnp.float32) * inverse
    cos_ref[...] = jnp.cos(angles)
    lane = lax.broadcasted_iota(jnp.int32, (span_len, HD), 1)
    sine = jnp.sin(angles)
    sin_ref[...] = jnp.where(lane < HD // 2, -sine, sine)

    def norm_rotate(v, gain, zb):
        place = pl.ds(pl.multiple_of(zb * chunk, chunk), chunk)
        v = v * lax.rsqrt(jnp.mean(v * v, axis=-1, keepdims=True) + epsilon) * gain
        return v * cos_ref[place, :] + pltpu.roll(v, HD // 2, 1) * sin_ref[place, :]

    kind = t // Z

    def kv_copy(zb, j):
        return pltpu.make_async_remote_copy(
            src_ref=kv_send.at[zb, j],
            dst_ref=kv_in.at[kind, pl.ds(pl.multiple_of(zb * chunk, chunk), chunk), :],
            send_sem=kv_ssem.at[zb, j],
            recv_sem=kv_rsem.at[kind, zb],
            device_id={"tensor": (2 * t + j) % (Z * X)},
            device_id_type=MESH,
        )

    def project(zb):
        place = pl.ds(pl.multiple_of(zb * chunk, chunk), chunk)
        rows = rows_ref[place, :]
        kv = jnp.dot(rows, wkv_t_ref[...], preferred_element_type=jnp.float32).astype(jnp.bfloat16)
        for j in range(2):
            kv_send[zb, j] = kv[:, j * HD : (j + 1) * HD]
            here = (2 * t + j) % (Z * X) == t

            @pl.when(here)
            def _():
                kv_in[kind, place, :] = kv_send[zb, j]

            @pl.when(jnp.logical_not(here))
            def _():
                kv_copy(zb, j).start()

        raw = jnp.dot(rows, wq_ref[...], preferred_element_type=jnp.float32)
        for j in range(2):
            q = norm_rotate(raw[:, j * HD : (j + 1) * HD], q_gain_ref[...][None], zb) * HD ** (-0.5)
            query_ref[zb, j * chunk : (j + 1) * chunk, :] = q.astype(jnp.bfloat16)

    weight_copies[1].wait()
    wkv_t_ref[...] = wkv_ref[...].T
    weight_copies[0].wait()
    for k in range(1, Z):
        for h in range(PIECES):
            row_copy(order[k], x, h, x_peer, row_x_send).wait_recv()
            forward(order[k], h)
        for done in ([], [0], [1, 2])[k - 1]:
            for h in range(PIECES):
                row_copy(order[done], 1 - x, h, x_peer, row_x_send).wait_recv()
            project(order[done])
    def pair_copy(index, zb, source, target):
        place = pl.ds(zb * chunk, chunk)
        return pltpu.make_async_remote_copy(
            src_ref=source.at[place, :],
            dst_ref=target.at[place, :],
            send_sem=pair_ssem.at[index, zb],
            recv_sem=pair_rsem.at[index, zb],
            device_id={"seq": 1 - s},
            device_id_type=MESH,
        )

    def kv_arrived(which, zb):
        @pl.when((t // 2 + which * Z) != t)
        def _():
            pltpu.make_async_remote_copy(
                src_ref=kv_send.at[zb, 0],
                dst_ref=kv_in.at[which, pl.ds(zb * chunk, chunk), :],
                send_sem=kv_ssem.at[zb, 0],
                recv_sem=kv_rsem.at[which, zb],
                device_id={"tensor": x_peer},
                device_id_type=MESH,
            ).wait_recv()

    values = kv_in.at[1]
    def share_keys(zb):
        kv_arrived(0, zb)
        place = slice(zb * chunk, (zb + 1) * chunk)
        raw = kv_in[0, place, :].astype(jnp.float32)
        key_own[place, :] = norm_rotate(raw, k_gain_ref[...][None], zb).astype(jnp.bfloat16)
        pair_copy(0, zb, key_own, key_other).start()
        kv_arrived(1, zb)
        pair_copy(1, zb, values, value_other).start()

    for zb in range(1, Z - 1):
        share_keys(zb)
    for h in range(PIECES):
        row_copy(order[Z - 1], 1 - x, h, x_peer, row_x_send).wait_recv()
    project(order[Z - 1])
    share_keys(0)
    share_keys(Z - 1)
    weight_copies[2].wait()
    for zb in range(Z):
        pair_copy(0, zb, key_own, key_other).wait_recv()
        pair_copy(1, zb, values, value_other).wait_recv()

    hide = jnp.where(span_ref[1 - s] < span_ref[s], 0.0, -1e30).astype(jnp.float32)

    def attend(zb):
        q = query_ref[zb]
        nt = (((1,), (1,)), ((), ()))
        mine = lax.dot_general(q, key_own[...], nt, preferred_element_type=jnp.float32)
        others = lax.dot_general(q, key_other[...], nt, preferred_element_type=jnp.float32) + hide
        row = lax.broadcasted_iota(jnp.int32, mine.shape, 0) % chunk + zb * chunk
        column = lax.broadcasted_iota(jnp.int32, mine.shape, 1)
        mine = jnp.where(column <= row, mine, -jnp.inf)
        largest = jnp.maximum(
            jnp.max(mine, axis=-1, keepdims=True), jnp.max(others, axis=-1, keepdims=True)
        )
        mine = jnp.exp(mine - largest)
        others = jnp.exp(others - largest)
        total = jnp.sum(mine, axis=-1, keepdims=True) + jnp.sum(others, axis=-1, keepdims=True)
        share = 1.0 / total
        result = jnp.dot(
            (mine * share).astype(jnp.bfloat16), kv_in[1], preferred_element_type=jnp.float32
        ) + jnp.dot(
            (others * share).astype(jnp.bfloat16), value_other[...], preferred_element_type=jnp.float32
        )
        result = result.astype(jnp.bfloat16)
        joined = jnp.concatenate([result[:chunk], result[chunk:]], axis=-1)
        part_ref[zb] = jnp.dot(joined, wo_ref[...], preferred_element_type=jnp.float32).astype(
            jnp.bfloat16
        )

    def part_copy(zb, h):
        place = pl.ds(pl.multiple_of((1 - x) * block + h * piece, piece), piece)
        return pltpu.make_async_remote_copy(
            src_ref=part_ref.at[zb, place, :],
            dst_ref=x_in.at[zb, pl.ds(h * piece, piece), :],
            send_sem=x_ssem.at[zb, h],
            recv_sem=x_rsem.at[zb, h],
            device_id={"tensor": x_peer},
            device_id_type=MESH,
        )

    def sum_copy(zb, h, target_ref, recv_sem, target):
        place = pl.ds(h * piece, piece)
        return pltpu.make_async_remote_copy(
            src_ref=line_out.at[zb, place, :],
            dst_ref=target_ref.at[zb, place, :],
            send_sem=line_ssem.at[zb, h],
            recv_sem=recv_sem.at[zb, h],
            device_id={"tensor": target},
            device_id_type=MESH,
        )

    def sum_up(zb, h):
        return sum_copy(zb, h, up_in, up_rsem, (t + X) % (Z * X))

    def sum_down(zb, h):
        return sum_copy(zb, h, down_in, down_rsem, (t + Z * X - X) % (Z * X))

    back = order[::-1]
    for zb in back:
        attend(zb)
        for h in range(PIECES):
            part_copy(zb, h).start()

    def pair_sum(zb, h):
        own_half = pl.ds(pl.multiple_of(x * block + h * piece, piece), piece)
        mine = part_ref[zb, own_half, :].astype(jnp.float32)
        return mine + x_in[zb, h * piece : (h + 1) * piece, :].astype(jnp.float32)

    def combine(zb, h):
        place = slice(h * piece, (h + 1) * piece)
        part_copy(zb, h).wait_recv()

        @pl.when(zb > z)
        def _():
            @pl.when(z > 0)
            def _():
                sum_up(zb, h).wait_recv()
                line_out[zb, place, :] = (
                    pair_sum(zb, h) + up_in[zb, place, :].astype(jnp.float32)
                ).astype(jnp.bfloat16)

            @pl.when(z == 0)
            def _():
                line_out[zb, place, :] = pair_sum(zb, h).astype(jnp.bfloat16)

            sum_up(zb, h).start()

        @pl.when(zb < z)
        def _():
            @pl.when(z < Z - 1)
            def _():
                sum_down(zb, h).wait_recv()
                line_out[zb, place, :] = (
                    pair_sum(zb, h) + down_in[zb, place, :].astype(jnp.float32)
                ).astype(jnp.bfloat16)

            @pl.when(z == Z - 1)
            def _():
                line_out[zb, place, :] = pair_sum(zb, h).astype(jnp.bfloat16)

            sum_down(zb, h).start()

    for zb in back[: Z - 1]:
        for h in range(PIECES):
            combine(zb, h)

    for h in range(PIECES):
        place = slice(h * piece, (h + 1) * piece)
        part_copy(z, h).wait_recv()
        total = hidden_ref[place, :].astype(jnp.float32) + pair_sum(z, h)

        @pl.when(z == 0)
        def _():
            sum_down(z, h).wait_recv()
            out_ref[place, :] = (total + down_in[z, place, :].astype(jnp.float32)).astype(jnp.bfloat16)

        @pl.when(z == Z - 1)
        def _():
            sum_up(z, h).wait_recv()
            out_ref[place, :] = (total + up_in[z, place, :].astype(jnp.float32)).astype(jnp.bfloat16)

        @pl.when((z > 0) & (z < Z - 1))
        def _():
            sum_down(z, h).wait_recv()
            sum_up(z, h).wait_recv()
            out_ref[place, :] = (
                total + down_in[z, place, :].astype(jnp.float32) + up_in[z, place, :].astype(jnp.float32)
            ).astype(jnp.bfloat16)

    for zb in range(Z):
        for h in range(PIECES):
            across(zb, h).wait_send()
            part_copy(zb, h).wait_send()

            @pl.when((zb <= z) & (z < Z - 1))
            def _():
                line_up(zb, h).wait_send()

            @pl.when((zb >= z) & (z > 0))
            def _():
                line_down(zb, h).wait_send()

            @pl.when(zb != z)
            def _():
                sum_up(zb, h).wait_send()

        pair_copy(0, zb, key_own, key_other).wait_send()
        pair_copy(1, zb, values, value_other).wait_send()
        for j in range(2):
            @pl.when((2 * t + j) % (Z * X) != t)
            def _():
                kv_copy(zb, j).wait_send()


def fused_body(hidden_in, span_order, norm_gain, w_query, w_keyval_t, q_gain, k_gain, w_out):
    _, block, width = hidden_in.shape
    chunk = X * block
    span_len = Z * chunk
    vmem = pl.BlockSpec(memory_space=pltpu.VMEM)
    hbm = pl.BlockSpec(memory_space=pltpu.HBM)
    bf16 = jnp.bfloat16
    dma = pltpu.SemaphoreType.DMA
    out = pl.pallas_call(
        layer_kernel,
        out_shape=jax.ShapeDtypeStruct((block, width), bf16),
        in_specs=[hbm] * 8,
        out_specs=vmem,
        scratch_shapes=[
            pltpu.SMEM(span_order.shape, jnp.int32),
            pltpu.VMEM((block, width), bf16),
            pltpu.VMEM(norm_gain.shape, jnp.float32),
            pltpu.VMEM(q_gain.shape, jnp.float32),
            pltpu.VMEM(k_gain.shape, jnp.float32),
            pltpu.VMEM((width, w_keyval_t.shape[0]), bf16),
            pltpu.VMEM((span_len, width), bf16),
            pltpu.VMEM(w_query.shape, bf16),
            pltpu.VMEM(w_keyval_t.shape, bf16),
            pltpu.VMEM(w_out.shape, bf16),
            pltpu.VMEM((span_len, HD), jnp.float32),
            pltpu.VMEM((span_len, HD), jnp.float32),
            pltpu.VMEM((Z, 2 * chunk, HD), bf16),
            pltpu.VMEM((Z, 2, chunk, HD), bf16),
            pltpu.VMEM((2, span_len, HD), bf16),
            pltpu.VMEM((span_len, HD), bf16),
            pltpu.VMEM((span_len, HD), bf16),
            pltpu.VMEM((span_len, HD), bf16),
            pltpu.VMEM((Z, chunk, width), bf16),
            pltpu.VMEM((Z, block, width), bf16),
            pltpu.VMEM((Z, block, width), bf16),
            pltpu.VMEM((Z, block, width), bf16),
            pltpu.VMEM((Z, block, width), bf16),
            dma((8,)),
            dma((Z * X, PIECES)),
            dma((Z, PIECES)),
            dma((Z, PIECES)),
            dma((Z, PIECES)),
            dma((Z, PIECES)),
            dma((2, Z)),
            dma((2, Z)),
            dma((2, Z)),
            dma((Z, PIECES)),
            dma((Z, PIECES)),
            dma((Z, PIECES)),
            dma((Z, PIECES)),
            dma((Z, PIECES)),
        ],
        compiler_params=pltpu.CompilerParams(
            collective_id=0, has_side_effects=True, vmem_limit_bytes=64 * 1024 * 1024
        ),
    )(
        span_order, hidden_in, norm_gain, q_gain, k_gain,
        w_query, w_keyval_t, w_out,
    )
    return out[None]


def solution(mesh):
    placed = (
        P(("groups", "seq"), "tensor", None),
        P("groups"),
        P(),
        P(None, "tensor"),
        P("tensor", None),
        P(),
        P(),
        P("tensor", None),
    )
    def chosen(hidden_in, span_order, norm_gain, w_query, *rest):
        fits = (
            mesh.shape["tensor"] == Z * X
            and mesh.shape["seq"] == 2
            and w_query.shape[1] == 2 * HD
            and hidden_in.shape[1] % (16 * PIECES) == 0
        )
        run = fused_body if fits else body
        return run(hidden_in, span_order, norm_gain, w_query, *rest)

    return jax.shard_map(
        chosen,
        mesh=mesh,
        in_specs=placed,
        out_specs=P(("groups", "seq"), "tensor", None),
        check_vma=False,
    )
```
